256 devices in a mesh: segment: 4 (over x), lat: 64 (over z, y, core).
Axes of the slice: x: 4, y: 4, z: 8, core: 2. Of those that a mesh axis runs over, the one named last changes fastest.
Arguments:
- tokens: bfloat16 [4, 4, 768, 6, 512], P(None, None, 'lat'), may hold values from -6 to 6
- norm_gain: float32 [4, 2, 512], P('segment'), may hold values from 0.25 to 1.75
- w_qkv: bfloat16 [4, 512, 1536], P('segment', 'lat'), may hold values from -2 to 2
- w_proj: bfloat16 [4, 512, 512], P('segment', 'lat'), may hold values from -0.25 to 0.25
- w_up: bfloat16 [4, 512, 2048], P('segment', 'lat'), may hold values from -0.25 to 0.25
- w_down: bfloat16 [4, 2048, 512], P('segment', 'lat'), may hold values from -0.125 to 0.125
Outputs:
- block_out: bfloat16 [4, 4, 4, 768, 6, 512], P('segment', None, None, 'lat')
The draws below stay inside these ranges and needn't reach their ends.
All inputs are finite; a program needn't handle non-finite values.
Results may differ from the reference program's by a relative error of at most 0.017.
Values may be sent and summed in bfloat16 or wider, within the bound.
No kernel may reach another device: no remote copies, remote signals or barrier semaphores. Data moves between devices by JAX's collectives and lax.ppermute only.
A program may use at most 64 MiB of HBM per device.

```python
import jax
import jax.numpy as jnp
from jax import lax

D = 512
HID = 2048
HEADS = 8
HEAD = 64
LEVELS = 4
LEVWIN = 2
ROWS = 12
HALF = 6
LONWIN = 6
LON = 6
MICRO = 4
LAT = 768


def draw_tokens(key, part):
    key = jax.random.fold_in(key, 5)
    base_key = jax.random.fold_in(key, 0)
    field = jax.random.normal(base_key, (MICRO, LEVELS, LAT, LON, D), jnp.float32)
    return jnp.clip(field, -6.0, 6.0).astype(jnp.bfloat16)


def draw_w_qkv(key, part):
    key = jax.random.fold_in(key, 7)
    base_key = jax.random.fold_in(key, 0)
    weight_scale = D ** (-0.5)
    weights = jnp.clip(jax.random.normal(base_key, (4, D, 3 * D), jnp.float32), -6.0, 6.0) * weight_scale
    return jnp.clip(weights, -2.0, 2.0).astype(jnp.bfloat16)


def block_scale(key, dims, pieces, smallest, top_value):
    factor_of, own = 1.0, jax.random.fold_in(key, 6)
    for dim, blocks in pieces:
        draws = jnp.exp(jax.random.uniform(jax.random.fold_in(own, dim), (blocks,), jnp.float32, smallest / len(pieces), top_value / len(pieces)))
        factor_of = factor_of * jnp.repeat(draws, dims[dim] // blocks).reshape([-1 if axis == dim else 1 for axis in range(len(dims))])
    return factor_of


def centred(rng, dims, scale, most, pieces=(), held_as=jnp.bfloat16):
    level = block_scale(rng, dims, pieces, -0.22, 0.18) if pieces else 1.0
    array = jax.random.normal(rng, dims, jnp.float32) * scale * level
    return jnp.minimum(jnp.maximum(array, -most), most).astype(held_as)


def setup_inputs(seed: int = 0) -> dict:
    splits = jax.random.split(jax.random.key(seed), 7)
    return {
        "tokens": draw_tokens(jax.random.fold_in(splits[6], 71), 0),
        "norm_gain": jnp.clip(1.0 + 0.15 * jax.random.normal(splits[1], (4, 2, D), jnp.float32), 0.25, 1.75),
        "w_qkv": draw_w_qkv(jax.random.fold_in(splits[6], 71), 0),
        "w_proj": centred(splits[3], (4, D, D), D ** -0.5, 0.25, ((0, 4), (1, 64))),
        "w_up": centred(splits[4], (4, D, HID), D ** -0.5, 0.25, ((0, 4), (1, 64))),
        "w_down": centred(splits[5], (4, HID, D), HID ** -0.5, 0.125, ((0, 4), (1, 64))),
    }


EPS = 1e-05

def layer_norm(values, gain):
    wide = values.astype(jnp.float32)
    center = lax.optimization_barrier(jnp.mean(wide, axis=-1, keepdims=True))
    spread = lax.optimization_barrier(jnp.mean(jnp.square(wide - center), axis=-1, keepdims=True))
    return (wide - center) * lax.rsqrt(spread + EPS) * gain

def to_windows(field, row_span):
    levels, rows_all, lons, width = field.shape
    shaped = field.reshape(levels // LEVWIN, LEVWIN, rows_all // row_span, row_span, lons // LONWIN, LONWIN, width)
    shaped = shaped.transpose(0, 2, 4, 1, 3, 5, 6)
    return shaped.reshape(levels // LEVWIN, rows_all // row_span, lons // LONWIN, LEVWIN * row_span * LONWIN, width)

def from_windows(field, row_span, rows_all, lons):
    width = field.shape[-1]
    shaped = field.reshape(LEVELS // LEVWIN, rows_all // row_span, lons // LONWIN, LEVWIN, row_span, LONWIN, width)
    shaped = shaped.transpose(0, 3, 1, 4, 2, 5, 6)
    return shaped.reshape(LEVELS, rows_all, lons, width)

def window_mask(query_region, key_region, key_valid, query_span, key_span):
    query_win = to_windows(query_region[..., None], query_span)[..., 0]
    key_win = to_windows(key_region[..., None], key_span)[..., 0]
    valid_win = to_windows(key_valid[..., None], key_span)[..., 0]
    return (query_win[..., :, None] == key_win[..., None, :]) & (valid_win[..., None, :] > 0)

def attend(queries, keys, values, allowed):
    query_heads = queries.reshape(queries.shape[:-1] + (HEADS, HEAD)).astype(jnp.float32)
    key_heads = keys.reshape(keys.shape[:-1] + (HEADS, HEAD)).astype(jnp.float32)
    value_heads = values.reshape(values.shape[:-1] + (HEADS, HEAD)).astype(jnp.float32)
    scores = jnp.einsum('abcqhe,abckhe->abchqk', query_heads, key_heads) * HEAD ** (-0.5)
    scores = jnp.where(allowed[:, :, :, None], scores, -1e+30)
    row_top = lax.optimization_barrier(jnp.max(scores, axis=-1, keepdims=True))
    expo_terms = jnp.exp(scores - row_top)
    probs = (expo_terms / lax.optimization_barrier(jnp.sum(expo_terms, axis=-1, keepdims=True))).astype(jnp.bfloat16)
    mixed = jnp.einsum('abchqk,abckhe->abcqhe', probs.astype(jnp.float32), value_heads)
    return mixed.reshape(mixed.shape[:-2] + (HEADS * HEAD,)).astype(jnp.bfloat16)

def swin_block(field, gains, proj_qkv, proj_out, proj_up, proj_down, shifted):
    rows_all, lons = (field.shape[1], field.shape[2])
    normed = layer_norm(field, gains[0]).astype(jnp.bfloat16)
    packed = jnp.dot(normed, proj_qkv, preferred_element_type=jnp.float32).astype(jnp.bfloat16)
    queries = packed[..., :D]
    keyvals = packed[..., D:]
    region = jnp.zeros((LEVELS,), jnp.int32)
    margin = 0
    if shifted:
        queries = jnp.roll(queries, -1, 0)
        keyvals = jnp.roll(keyvals, -1, 0)
        region = (jnp.arange(LEVELS) == LEVELS - 1).astype(jnp.int32)
        margin = HALF
        queries = jnp.pad(queries, ((0, 0), (HALF, HALF), (0, 0), (0, 0)))
        keyvals = jnp.pad(keyvals, ((0, 0), (HALF, HALF), (0, 0), (0, 0)))
    padded_rows = rows_all + 2 * margin
    row_ids = jnp.arange(padded_rows)
    row_valid = ((row_ids >= margin) & (row_ids < margin + rows_all)).astype(jnp.int32)
    region_map = jnp.broadcast_to(region[:, None, None], (LEVELS, padded_rows, lons))
    valid_map = jnp.broadcast_to(row_valid[None, :, None], (LEVELS, padded_rows, lons))
    allowed = window_mask(region_map, region_map, valid_map, ROWS, ROWS)
    key_win = to_windows(keyvals, ROWS)
    mixed = attend(to_windows(queries, ROWS), key_win[..., :D], key_win[..., D:], allowed)
    mixed = from_windows(mixed, ROWS, padded_rows, lons)
    if shifted:
        mixed = jnp.roll(mixed[:, HALF:HALF + rows_all], 1, 0)
    residual = field.astype(jnp.float32) + jnp.dot(mixed, proj_out, preferred_element_type=jnp.float32)
    inner_norm = layer_norm(residual, gains[1]).astype(jnp.bfloat16)
    hidden = jax.nn.gelu(jnp.dot(inner_norm, proj_up, preferred_element_type=jnp.float32)).astype(jnp.bfloat16)
    return (residual + jnp.dot(hidden, proj_down, preferred_element_type=jnp.float32)).astype(jnp.bfloat16)

def reference(tokens, norm_gain, w_qkv, w_proj, w_up, w_down):

    def run_block(field, block_index):
        return swin_block(field, norm_gain[block_index], w_qkv[block_index], w_proj[block_index], w_up[block_index], w_down[block_index], block_index % 2 == 1)
    results = []
    for micro_index in range(MICRO):
        first_out = run_block(tokens[micro_index], 0)
        second_out = run_block(first_out, 1)
        third_out = run_block(second_out, 2)
        joined = (third_out.astype(jnp.float32) + first_out.astype(jnp.float32)).astype(jnp.bfloat16)
        fourth_out = run_block(joined, 3)
        results.append(jnp.stack([first_out, second_out, third_out, fourth_out]))
    return jnp.stack(results, axis=1)
```

```python
import jax
import jax.numpy as jnp
from jax import lax
from jax.experimental import pallas as pl
from jax.experimental.pallas import tpu as pltpu
from jax.sharding import PartitionSpec as P

D = 512
LEVELS = 4
HALFROWS = 144
OWN = 288
PER_LEVEL = 36
EPS = 1e-5


def layer_norm(wide, gain):
    center = jnp.mean(wide, axis=-1, keepdims=True)
    moved = wide - center
    spread = jnp.mean(moved * moved, axis=-1, keepdims=True)
    return moved * lax.rsqrt(spread + EPS) * gain


def dot(a, b):
    return jnp.dot(a, b, preferred_element_type=jnp.float32)


def attention(q, k, v, bias, first_lane, ones):
    zero = jnp.zeros_like(q)
    stacked = jnp.concatenate([jnp.where(first_lane, q, zero), jnp.where(first_lane, zero, q)], axis=0)
    scores = lax.dot_general(stacked, k, (((1,), (1,)), ((), ())), preferred_element_type=jnp.float32)
    scores = scores + bias
    top = jnp.max(scores, axis=-1, keepdims=True)
    terms = jnp.exp(scores - top).astype(jnp.bfloat16)
    both = dot(terms, jnp.concatenate([v, ones], axis=1))
    rows = q.shape[0]
    weighed = jnp.where(first_lane, both[:rows, :128], both[rows:, :128])
    total = jnp.where(first_lane, both[:rows, 128:], both[rows:, 128:])
    return (weighed / total).astype(jnp.bfloat16)


def half_bias(shifted, half, has_prev, has_next):
    row = lax.broadcasted_iota(jnp.int32, (HALFROWS, OWN), 0)
    col = lax.broadcasted_iota(jnp.int32, (HALFROWS, OWN), 1)
    far = col >= HALFROWS
    key = jnp.where(far, col - HALFROWS, col)

    def level(i):
        return ((i >= PER_LEVEL).astype(jnp.int32) + (i >= 2 * PER_LEVEL).astype(jnp.int32)
                + (i >= 3 * PER_LEVEL).astype(jnp.int32))

    row_level, key_level = level(row), level(key)
    if shifted:
        group = lambda l: jnp.where(l == 2, 1, l)
        allowed = group(row_level) == group(key_level)
        if half == 0:
            allowed = allowed & (far | (has_prev > 0))
        else:
            allowed = allowed & (jnp.logical_not(far) | (has_next > 0))
    else:
        group = lambda l: (l >= 2).astype(jnp.int32)
        allowed = group(row_level) == group(key_level)
    return jnp.where(allowed, 0.0, -1e30).astype(jnp.float32)


def block_kernel(shifted, joins, wait_weights, edge_ref, refs, gain_ref, w, out_refs, mixed_ref):
    own = refs["own"][...].astype(jnp.float32)
    gain0 = gain_ref[0:1, :]
    normed = layer_norm(own, gain0).astype(jnp.bfloat16)
    if shifted:
        before = layer_norm(refs["prev"][...].astype(jnp.float32), gain0).astype(jnp.bfloat16)
        after = layer_norm(refs["next"][...].astype(jnp.float32), gain0).astype(jnp.bfloat16)
        around = jnp.concatenate([before, normed, after], axis=0)
    else:
        around = normed
    wait_weights("q")
    q = (dot(normed, w["q"]()) ).astype(jnp.bfloat16) * jnp.bfloat16(0.125)
    wait_weights("k")
    k = dot(around, w["k"]()).astype(jnp.bfloat16)
    wait_weights("v")
    v = dot(around, w["v"]()).astype(jnp.bfloat16)
    first_lane = lax.broadcasted_iota(jnp.int32, (HALFROWS, 128), 1) < 64
    ones = jnp.ones((OWN, 128), jnp.bfloat16)
    for half in range(2):
        bias = half_bias(shifted, half, edge_ref[0], edge_ref[1])
        bias = jnp.concatenate([bias, bias], axis=0)
        rows = slice(half * HALFROWS, (half + 1) * HALFROWS)
        start = half * OWN if shifted else 0
        keys = slice(start, start + OWN)
        for pair in range(4):
            cols = slice(pair * 128, (pair + 1) * 128)
            mixed_ref[rows, cols] = attention(q[rows, cols], k[keys, cols], v[keys, cols], bias, first_lane, ones)
    wait_weights("proj")
    residual = own + dot(mixed_ref[...], w["proj"]())
    inner = layer_norm(residual, gain_ref[1:2, :]).astype(jnp.bfloat16)
    total = residual
    for t in range(4):
        wait_weights("up%d" % t)
        hidden = jax.nn.gelu(dot(inner, w["up%d" % t]())).astype(jnp.bfloat16)
        if t == 0:
            wait_weights("down")
        total = total + dot(hidden, w["down"](t))
    result = total.astype(jnp.bfloat16)
    out_refs[0][...] = result
    if joins:
        out_refs[1][...] = (result.astype(jnp.float32) + refs["skip"][...].astype(jnp.float32)).astype(jnp.bfloat16)


ZS, YS = 8, 4
LATS = 2 * ZS * YS
PAIRS = [(0, 3), (1, 2)]


def run_block(weights, x, gains, edges, halo=None, skip=None):
    shifted = halo is not None
    joins = skip is not None
    operands = {"own": x}
    if shifted:
        operands["prev"], operands["next"] = halo
    if joins:
        operands["skip"] = skip
    names = list(operands)
    outs = 2 if joins else 1
    order = ("q", "k", "v", "proj", "up0", "up1", "up2", "up3")

    def body(edge_ref, gain_ref, w_ref, *rest):
        refs = dict(zip(names, rest[: len(names)]))
        out_refs = rest[len(names) : len(names) + outs]
        tiles, mixed, sems = rest[len(names) + outs :]
        copies = {}
        for i, name in enumerate(order):
            copies[name] = pltpu.make_async_copy(w_ref.at[i], tiles.at[i], sems.at[i])
        copies["down"] = pltpu.make_async_copy(w_ref.at[pl.ds(8, 4)], tiles.at[pl.ds(8, 4)], sems.at[8])
        for copy in copies.values():
            copy.start()
        w = {name: (lambda i=i: tiles[i].reshape(D, D)) for i, name in enumerate(order)}
        w["down"] = lambda t: jnp.concatenate(
            [tiles[8 + u, 8 * t + j] for j in range(8) for u in range(4)], axis=0
        )
        block_kernel(shifted, joins, lambda name: copies[name].wait(), edge_ref, refs, gain_ref, w, out_refs, mixed)

    vmem = pl.BlockSpec(memory_space=pltpu.VMEM)
    shape = jax.ShapeDtypeStruct((OWN, D), jnp.bfloat16)
    result = pl.pallas_call(
        body,
        out_shape=(shape,) * outs,
        in_specs=[pl.BlockSpec(memory_space=pltpu.SMEM), vmem, pl.BlockSpec(memory_space=pl.ANY)]
        + [vmem] * len(names),
        out_specs=(vmem,) * outs,
        scratch_shapes=[
            pltpu.VMEM((12, 32, 16, D), jnp.bfloat16),
            pltpu.VMEM((OWN, D), jnp.bfloat16),
            pltpu.SemaphoreType.DMA((9,)),
        ],
        compiler_params=pltpu.CompilerParams(vmem_limit_bytes=32 * 1024 * 1024),
        cost_estimate=pl.CostEstimate(flops=5 * 10**9, bytes_accessed=7 * 10**6, transcendentals=10**6),
    )(edges, gains, weights, *operands.values())
    return result if joins else result[0]


def assemble(place, mine, passed):
    def body(place_ref, *rest):
        out, sems = rest[10], rest[11]
        z0, y0, core = place_ref[0], place_ref[1], place_ref[2]
        copies = []
        for side in range(2):
            source_core = core if side == 0 else 1 - core
            base = 6 * source_core
            for piece, outer in enumerate((0, -1, 1, -2, 2)):
                ref = rest[5 * side + piece]
                inner_first = 2 if piece == 4 else 0
                inner_count = ref.shape[0]
                for n in range(inner_count):
                    inner = inner_first + n
                    parts = ((0, 3, -2), (3, 3, 2)) if inner == 3 else ((0, 6, (0, -1, 1)[inner]),)
                    for first, count, step in parts:
                        for far in range(2):
                            z_step = jnp.where(source_core == 0, step, outer) + 4 * far
                            y_step = jnp.where(source_core == 0, outer, step)
                            chip = lax.rem(z0 + z_step + ZS, ZS) * YS + lax.rem(y0 + y_step + YS, YS)
                            copies.append(
                                pltpu.make_async_copy(
                                    ref.at[n, far, pl.ds(first, count)],
                                    out.at[pl.ds(base + first, count), chip],
                                    sems.at[len(copies)],
                                )
                            )
        for copy in copies:
            copy.start()
        for copy in copies:
            copy.wait()

    anywhere = pl.BlockSpec(memory_space=pl.ANY)
    return pl.pallas_call(
        body,
        out_shape=jax.ShapeDtypeStruct((12, 32, 16, D), jnp.bfloat16),
        in_specs=[pl.BlockSpec(memory_space=pltpu.SMEM)] + [anywhere] * 10,
        out_specs=anywhere,
        scratch_shapes=[pltpu.SemaphoreType.DMA((80,))],
        cost_estimate=pl.CostEstimate(flops=10**6, bytes_accessed=13 * 10**6, transcendentals=0),
    )(place, *mine, *passed)


def lat_id(z, y, core):
    return ((z % ZS) * YS + y % YS) * 2 + core


def moved(along):
    pairs = []
    for z in range(ZS):
        for y in range(YS):
            for core in range(2):
                dz, dy = along(core)
                pairs.append((lat_id(z, y, core), lat_id(z + dz, y + dy, core)))
    return pairs


def ring(level, step):
    return moved(lambda core: (step, 0) if (level == 0) == (core == 0) else (0, step))


SWAP = [(i, i ^ 1) for i in range(LATS)]


def send(value, pairs):
    return lax.ppermute(value, "lat", pairs)


def gather_weights(place, shard):
    both = jnp.stack([shard, send(shard, moved(lambda core: (4, 0)))])
    before, after = send(both, ring(0, 1)), send(both, ring(0, -1))
    far = jnp.concatenate([send(before[:, :3], ring(0, 1)), send(after[:, 3:], ring(0, -1))], axis=1)
    line = jnp.stack([both, before, after, far])
    before, after = send(line, ring(1, 1)), send(line, ring(1, -1))
    mine = [line, before, after, send(before[:2], ring(1, 1)), send(after[2:], ring(1, -1))]
    return assemble(place, mine, [send(piece, SWAP) for piece in mine])


def on_device(tokens, norm_gain, w_qkv, w_proj, w_up, w_down):
    segment = lax.axis_index("segment")
    lat = lax.axis_index("lat")
    core = lat % 2
    even = segment % 2 == 0
    low = (segment == 0) | (segment == 3)
    place = jnp.stack([lat // (2 * YS), (lat // 2) % YS, core]).astype(jnp.int32)
    edges = jnp.stack([lat > 0, lat < LATS - 1]).astype(jnp.int32)

    own = jnp.concatenate(
        [w_qkv[0, :, i * D : (i + 1) * D] for i in range(3)]
        + [w_proj[0]]
        + [w_up[0, :, i * D : (i + 1) * D] for i in range(4)]
        + [w_down[0]],
        axis=0,
    )
    other = send(own, SWAP)
    first, second = jnp.where(core == 0, own, other), jnp.where(core == 0, other, own)
    tall = jnp.stack([first[:64].reshape(8, 8, D), second[:64].reshape(8, 8, D)], axis=1).reshape(8, 16, D)
    tall = jnp.concatenate([tall, first[64:].reshape(2, 16, D), second[64:].reshape(2, 16, D)], axis=0)
    shard = jnp.where(core == 0, tall[:6], tall[6:])
    beside = [(0, 1), (1, 0), (2, 3), (3, 2)]
    other = lax.ppermute(shard, "segment", beside)
    other_gain = lax.ppermute(norm_gain[0], "segment", beside)
    weights = [
        gather_weights(place, jnp.where(even, shard, other)),
        gather_weights(place, jnp.where(even, other, shard)),
    ]
    gains = [jnp.where(even, norm_gain[0], other_gain), jnp.where(even, other_gain, norm_gain[0])]

    fields = jnp.where(low, tokens[:2], tokens[2:])
    fields = fields.reshape(2, LEVELS, 2, 6, 6, D).transpose(0, 2, 1, 3, 4, 5).reshape(2, OWN, D)

    def halo(field):
        up = send(field[HALFROWS:], [(i, i + 1) for i in range(LATS - 1)])
        down = send(field[:HALFROWS], [(i + 1, i) for i in range(LATS - 1)])
        return up, down

    def pass_on(value, pairs):
        return lax.ppermute(value, "segment", pairs)

    pair = range(2)
    a0 = [run_block(weights[0], fields[m], gains[0], edges) for m in pair]
    a1 = [run_block(weights[1], a0[m], gains[1], edges, halo=halo(a0[m])) for m in pair]
    skips = [pass_on(a0[m], PAIRS) for m in pair]
    entering = [pass_on(a1[m], PAIRS) for m in pair]
    a2, a3 = [], []
    for m in pair:
        out, joined = run_block(weights[0], entering[m], gains[0], edges, skip=skips[m])
        a2.append((out, joined))
    for m in pair:
        a3.append(run_block(weights[1], a2[m][1], gains[1], edges, halo=halo(a2[m][1])))
    a2 = [out for out, _ in a2]

    def select(b0, b1, b2, b3):
        return jnp.where(segment == 0, b0, jnp.where(segment == 1, b1, jnp.where(segment == 2, b2, b3)))

    kept, got = [], []
    for m in pair:
        kept.append(select(a0[m], a1[m], a2[m], a3[m]))
        got.append(
            select(
                pass_on(a0[m], [(1, 0)]),
                pass_on(a1[m], [(0, 1)]),
                pass_on(a2[m], [(3, 2)]),
                pass_on(a3[m], [(2, 3)]),
            )
        )
    outs = [jnp.where(low, kept[m], got[m]) for m in pair] + [jnp.where(low, got[m], kept[m]) for m in pair]
    out = jnp.stack(outs).reshape(4, 2, LEVELS, 6, 6, D).transpose(0, 2, 1, 3, 4, 5)
    return out.reshape(1, 4, LEVELS, 12, 6, D)


def solution(mesh):
    return jax.shard_map(
        on_device,
        mesh=mesh,
        in_specs=(
            P(None, None, "lat", None, None),
            P("segment", None, None),
            P("segment", "lat", None),
            P("segment", "lat", None),
            P("segment", "lat", None),
            P("segment", "lat", None),
        ),
        out_specs=P("segment", None, None, "lat", None, None),
        check_vma=False,
    )
```

```python
import jax
import jax.numpy as jnp
from jax import lax
from jax.experimental import pallas as pl
from jax.experimental.pallas import tpu as pltpu
from jax.sharding import PartitionSpec as P

D = 512
LEVELS = 4
HALFROWS = 144
OWN = 288
PER_LEVEL = 36
EPS = 1e-5


def layer_norm(wide, gain):
    center = jnp.mean(wide, axis=-1, keepdims=True)
    moved = wide - center
    spread = jnp.mean(moved * moved, axis=-1, keepdims=True)
    return moved * lax.rsqrt(spread + EPS) * gain


def dot(a, b):
    return jnp.dot(a, b, preferred_element_type=jnp.float32)


def attention(q, k, v, bias, first_lane, ones):
    zero = jnp.zeros_like(q)
    stacked = jnp.concatenate([jnp.where(first_lane, q, zero), jnp.where(first_lane, zero, q)], axis=0)
    scores = lax.dot_general(stacked, k, (((1,), (1,)), ((), ())), preferred_element_type=jnp.float32)
    scores = scores + bias
    top = jnp.max(scores, axis=-1, keepdims=True)
    terms = jnp.exp(scores - top).astype(jnp.bfloat16)
    both = dot(terms, jnp.concatenate([v, ones], axis=1))
    rows = q.shape[0]
    weighed = jnp.where(first_lane, both[:rows, :128], both[rows:, :128])
    total = jnp.where(first_lane, both[:rows, 128:], both[rows:, 128:])
    return (weighed / total).astype(jnp.bfloat16)


def half_bias(shifted, half, has_prev, has_next):
    row = lax.broadcasted_iota(jnp.int32, (HALFROWS, OWN), 0)
    col = lax.broadcasted_iota(jnp.int32, (HALFROWS, OWN), 1)
    far = col >= HALFROWS
    key = jnp.where(far, col - HALFROWS, col)

    def level(i):
        return ((i >= PER_LEVEL).astype(jnp.int32) + (i >= 2 * PER_LEVEL).astype(jnp.int32)
                + (i >= 3 * PER_LEVEL).astype(jnp.int32))

    row_level, key_level = level(row), level(key)
    if shifted:
        group = lambda l: jnp.where(l == 2, 1, l)
        allowed = group(row_level) == group(key_level)
        if half == 0:
            allowed = allowed & (far | (has_prev > 0))
        else:
            allowed = allowed & (jnp.logical_not(far) | (has_next > 0))
    else:
        group = lambda l: (l >= 2).astype(jnp.int32)
        allowed = group(row_level) == group(key_level)
    return jnp.where(allowed, 0.0, -1e30).astype(jnp.float32)


def block_kernel(shifted, joins, wait_weights, edge_ref, refs, gain_ref, w, out_refs, mixed_ref):
    own = refs["own"][...].astype(jnp.float32)
    gain0 = gain_ref[0:1, :]
    normed = layer_norm(own, gain0).astype(jnp.bfloat16)
    if shifted:
        before = layer_norm(refs["prev"][...].astype(jnp.float32), gain0).astype(jnp.bfloat16)
        after = layer_norm(refs["next"][...].astype(jnp.float32), gain0).astype(jnp.bfloat16)
        around = jnp.concatenate([before, normed, after], axis=0)
    else:
        around = normed
    wait_weights("q")
    q = (dot(normed, w["q"]()) ).astype(jnp.bfloat16) * jnp.bfloat16(0.125)
    wait_weights("k")
    k = dot(around, w["k"]()).astype(jnp.bfloat16)
    wait_weights("v")
    v = dot(around, w["v"]()).astype(jnp.bfloat16)
    first_lane = lax.broadcasted_iota(jnp.int32, (HALFROWS, 128), 1) < 64
    ones = jnp.ones((OWN, 128), jnp.bfloat16)
    for half in range(2):
        bias = half_bias(shifted, half, edge_ref[0], edge_ref[1])
        bias = jnp.concatenate([bias, bias], axis=0)
        rows = slice(half * HALFROWS, (half + 1) * HALFROWS)
        start = half * OWN if shifted else 0
        keys = slice(start, start + OWN)
        for pair in range(4):
            cols = slice(pair * 128, (pair + 1) * 128)
            mixed_ref[rows, cols] = attention(q[rows, cols], k[keys, cols], v[keys, cols], bias, first_lane, ones)
    wait_weights("proj")
    residual = own + dot(mixed_ref[...], w["proj"]())
    inner = layer_norm(residual, gain_ref[1:2, :]).astype(jnp.bfloat16)
    total = residual
    for t in range(4):
        wait_weights("up%d" % t)
        hidden = jax.nn.gelu(dot(inner, w["up%d" % t]())).astype(jnp.bfloat16)
        if t == 0:
            wait_weights("down")
        total = total + dot(hidden, w["down"](t))
    result = total.astype(jnp.bfloat16)
    out_refs[0][...] = result
    if joins:
        out_refs[1][...] = (result.astype(jnp.float32) + refs["skip"][...].astype(jnp.float32)).astype(jnp.bfloat16)


ZS, YS = 8, 4
LATS = 2 * ZS * YS
PAIRS = [(0, 3), (1, 2)]


def run_block(weights, x, gains, edges, halo=None, skip=None):
    shifted = halo is not None
    joins = skip is not None
    operands = {"own": x}
    if shifted:
        operands["prev"], operands["next"] = halo
    if joins:
        operands["skip"] = skip
    names = list(operands)
    outs = 2 if joins else 1
    order = ("q", "k", "v", "proj", "up0", "up1", "up2", "up3")

    def body(edge_ref, gain_ref, tiles, *rest):
        refs = dict(zip(names, rest[: len(names)]))
        out_refs = rest[len(names) : len(names) + outs]
        mixed = rest[len(names) + outs]
        w = {name: (lambda i=i: tiles[i].reshape(D, D)) for i, name in enumerate(order)}
        w["down"] = lambda t: jnp.concatenate(
            [tiles[8 + u, 8 * t + j] for j in range(8) for u in range(4)], axis=0
        )
        block_kernel(shifted, joins, lambda name: None, edge_ref, refs, gain_ref, w, out_refs, mixed)

    vmem = pl.BlockSpec(memory_space=pltpu.VMEM)
    shape = jax.ShapeDtypeStruct((OWN, D), jnp.bfloat16)
    result = pl.pallas_call(
        body,
        out_shape=(shape,) * outs,
        in_specs=[pl.BlockSpec(memory_space=pltpu.SMEM), vmem, vmem] + [vmem] * len(names),
        out_specs=(vmem,) * outs,
        scratch_shapes=[pltpu.VMEM((OWN, D), jnp.bfloat16)],
        compiler_params=pltpu.CompilerParams(vmem_limit_bytes=24 * 1024 * 1024),
        cost_estimate=pl.CostEstimate(flops=5 * 10**9, bytes_accessed=7 * 10**6, transcendentals=10**6),
    )(edges, gains, pltpu.with_memory_space_constraint(weights, pltpu.VMEM), *operands.values())
    return result if joins else result[0]


def assemble(place, mine, passed):
    def body(place_ref, *rest):
        out = rest[10]
        z0, y0, core = place_ref[0], place_ref[1], place_ref[2]
        for side in range(2):
            source_core = core if side == 0 else 1 - core
            base = 6 * source_core
            for piece, outer in enumerate((0, -1, 1, -2, 2)):
                ref = rest[5 * side + piece]
                inner_first = 2 if piece == 4 else 0
                for n in range(ref.shape[0]):
                    inner = inner_first + n
                    parts = ((0, 3, -2), (3, 3, 2)) if inner == 3 else ((0, 6, (0, -1, 1)[inner]),)
                    for first, count, step in parts:
                        for far in range(2):
                            z_step = jnp.where(source_core == 0, step, outer) + 4 * far
                            y_step = jnp.where(source_core == 0, outer, step)
                            chip = lax.rem(z0 + z_step + ZS, ZS) * YS + lax.rem(y0 + y_step + YS, YS)
                            for tile in range(first, first + count):
                                out[base + tile, chip] = ref[n, far, tile]

    vmem = pl.BlockSpec(memory_space=pltpu.VMEM)
    return pl.pallas_call(
        body,
        out_shape=pltpu.VMEM((12, 32, 16, D), jnp.bfloat16),
        in_specs=[pl.BlockSpec(memory_space=pltpu.SMEM)] + [vmem] * 10,
        out_specs=vmem,
        compiler_params=pltpu.CompilerParams(vmem_limit_bytes=24 * 1024 * 1024),
        cost_estimate=pl.CostEstimate(flops=10**9, bytes_accessed=6 * 10**6, transcendentals=0),
    )(place, *mine, *passed)


def lat_id(z, y, core):
    return ((z % ZS) * YS + y % YS) * 2 + core


def moved(along):
    pairs = []
    for z in range(ZS):
        for y in range(YS):
            for core in range(2):
                dz, dy = along(core)
                pairs.append((lat_id(z, y, core), lat_id(z + dz, y + dy, core)))
    return pairs


def ring(level, step):
    return moved(lambda core: (step, 0) if (level == 0) == (core == 0) else (0, step))


SWAP = [(i, i ^ 1) for i in range(LATS)]


def send(value, pairs):
    return lax.ppermute(value, "lat", pairs)


def gather_weights(place, shard):
    both = jnp.stack([shard, send(shard, moved(lambda core: (4, 0)))])
    before, after = send(both, ring(0, 1)), send(both, ring(0, -1))
    far = jnp.concatenate([send(before[:, :3], ring(0, 1)), send(after[:, 3:], ring(0, -1))], axis=1)
    line = jnp.stack([both, before, after, far])
    before, after = send(line, ring(1, 1)), send(line, ring(1, -1))
    mine = [line, before, after, send(before[:2], ring(1, 1)), send(after[2:], ring(1, -1))]
    return assemble(place, mine, [send(piece, SWAP) for piece in mine])


def on_device(tokens, norm_gain, w_qkv, w_proj, w_up, w_down):
    segment = lax.axis_index("segment")
    lat = lax.axis_index("lat")
    core = lat % 2
    even = segment % 2 == 0
    low = (segment == 0) | (segment == 3)
    place = jnp.stack([lat // (2 * YS), (lat // 2) % YS, core]).astype(jnp.int32)
    edges = jnp.stack([lat > 0, lat < LATS - 1]).astype(jnp.int32)

    own = jnp.concatenate(
        [w_qkv[0, :, i * D : (i + 1) * D] for i in range(3)]
        + [w_proj[0]]
        + [w_up[0, :, i * D : (i + 1) * D] for i in range(4)]
        + [w_down[0]],
        axis=0,
    )
    other = send(own, SWAP)
    first, second = jnp.where(core == 0, own, other), jnp.where(core == 0, other, own)
    tall = jnp.stack([first[:64].reshape(8, 8, D), second[:64].reshape(8, 8, D)], axis=1).reshape(8, 16, D)
    tall = jnp.concatenate([tall, first[64:].reshape(2, 16, D), second[64:].reshape(2, 16, D)], axis=0)
    shard = jnp.where(core == 0, tall[:6], tall[6:])
    beside = [(0, 1), (1, 0), (2, 3), (3, 2)]
    other = lax.ppermute(shard, "segment", beside)
    other_gain = lax.ppermute(norm_gain[0], "segment", beside)
    weights = [
        gather_weights(place, jnp.where(even, shard, other)),
        gather_weights(place, jnp.where(even, other, shard)),
    ]
    gains = [jnp.where(even, norm_gain[0], other_gain), jnp.where(even, other_gain, norm_gain[0])]

    fields = jnp.where(low, tokens[:2], tokens[2:])
    fields = fields.reshape(2, LEVELS, 2, 6, 6, D).transpose(0, 2, 1, 3, 4, 5).reshape(2, OWN, D)

    def halo(field):
        up = send(field[HALFROWS:], [(i, i + 1) for i in range(LATS - 1)])
        down = send(field[:HALFROWS], [(i + 1, i) for i in range(LATS - 1)])
        return up, down

    def pass_on(value, pairs):
        return lax.ppermute(value, "segment", pairs)

    pair = range(2)
    a0 = [run_block(weights[0], fields[m], gains[0], edges) for m in pair]
    a1 = [run_block(weights[1], a0[m], gains[1], edges, halo=halo(a0[m])) for m in pair]
    skips = [pass_on(a0[m], PAIRS) for m in pair]
    entering = [pass_on(a1[m], PAIRS) for m in pair]
    a2, a3 = [], []
    for m in pair:
        out, joined = run_block(weights[0], entering[m], gains[0], edges, skip=skips[m])
        a2.append((out, joined))
    for m in pair:
        a3.append(run_block(weights[1], a2[m][1], gains[1], edges, halo=halo(a2[m][1])))
    a2 = [out for out, _ in a2]

    def select(b0, b1, b2, b3):
        return jnp.where(segment == 0, b0, jnp.where(segment == 1, b1, jnp.where(segment == 2, b2, b3)))

    kept, got = [], []
    for m in pair:
        kept.append(select(a0[m], a1[m], a2[m], a3[m]))
        got.append(
            select(
                pass_on(a0[m], [(1, 0)]),
                pass_on(a1[m], [(0, 1)]),
                pass_on(a2[m], [(3, 2)]),
                pass_on(a3[m], [(2, 3)]),
            )
        )
    outs = [jnp.where(low, kept[m], got[m]) for m in pair] + [jnp.where(low, got[m], kept[m]) for m in pair]
    out = jnp.stack(outs).reshape(4, 2, LEVELS, 6, 6, D).transpose(0, 2, 1, 3, 4, 5)
    return out.reshape(1, 4, LEVELS, 12, 6, D)


def solution(mesh):
    return jax.shard_map(
        on_device,
        mesh=mesh,
        in_specs=(
            P(None, None, "lat", None, None),
            P("segment", None, None),
            P("segment", "lat", None),
            P("segment", "lat", None),
            P("segment", "lat", None),
            P("segment", "lat", None),
        ),
        out_specs=P("segment", None, None, "lat", None, None),
        check_vma=False,
    )
```

```python
import jax
import jax.numpy as jnp
from jax import lax
from jax.experimental import pallas as pl
from jax.experimental.pallas import tpu as pltpu
from jax.sharding import PartitionSpec as P

D = 512
LEVELS = 4
HALFROWS = 144
OWN = 288
PER_LEVEL = 36
EPS = 1e-5


def layer_norm(wide, gain):
    center = jnp.mean(wide, axis=-1, keepdims=True)
    moved = wide - center
    spread = jnp.mean(moved * moved, axis=-1, keepdims=True)
    return moved * lax.rsqrt(spread + EPS) * gain


def dot(a, b):
    return jnp.dot(a, b, preferred_element_type=jnp.float32)


def attention(q, k, v, bias, first_lane, ones):
    zero = jnp.zeros_like(q)
    stacked = jnp.concatenate([jnp.where(first_lane, q, zero), jnp.where(first_lane, zero, q)], axis=0)
    scores = lax.dot_general(stacked, k, (((1,), (1,)), ((), ())), preferred_element_type=jnp.float32)
    scores = scores + bias
    top = jnp.max(scores, axis=-1, keepdims=True)
    terms = jnp.exp(scores - top).astype(jnp.bfloat16)
    both = dot(terms, jnp.concatenate([v, ones], axis=1))
    rows = q.shape[0]
    weighed = jnp.where(first_lane, both[:rows, :128], both[rows:, :128])
    total = jnp.where(first_lane, both[:rows, 128:], both[rows:, 128:])
    return (weighed / total).astype(jnp.bfloat16)


def half_bias(shifted, half, has_prev, has_next):
    row = lax.broadcasted_iota(jnp.int32, (HALFROWS, OWN), 0)
    col = lax.broadcasted_iota(jnp.int32, (HALFROWS, OWN), 1)
    far = col >= HALFROWS
    key = jnp.where(far, col - HALFROWS, col)

    def level(i):
        return ((i >= PER_LEVEL).astype(jnp.int32) + (i >= 2 * PER_LEVEL).astype(jnp.int32)
                + (i >= 3 * PER_LEVEL).astype(jnp.int32))

    row_level, key_level = level(row), level(key)
    if shifted:
        group = lambda l: jnp.where(l == 2, 1, l)
        allowed = group(row_level) == group(key_level)
        if half == 0:
            allowed = allowed & (far | (has_prev > 0))
        else:
            allowed = allowed & (jnp.logical_not(far) | (has_next > 0))
    else:
        group = lambda l: (l >= 2).astype(jnp.int32)
        allowed = group(row_level) == group(key_level)
    return jnp.where(allowed, 0.0, -1e30).astype(jnp.float32)


def block_kernel(shifted, joins, count, edge_ref, refs, gain_ref, tiles, outs, mixed_ref):
    names = ("q", "k", "v", "proj", "up0", "up1", "up2", "up3")
    w = {name: (lambda i=i: tiles[i].reshape(D, D)) for i, name in enumerate(names)}

    def load(name):
        ref, index = refs[name]
        if index is None:
            return ref[...].reshape(-1, D).astype(jnp.float32)
        return ref[index].astype(jnp.float32)

    own = load("own")
    gain0 = gain_ref[0:1, :]
    normed = layer_norm(own, gain0).astype(jnp.bfloat16)
    if shifted:
        before = layer_norm(load("prev"), gain0).astype(jnp.bfloat16)
        after = layer_norm(load("next"), gain0).astype(jnp.bfloat16)
        around = jnp.concatenate([before, normed, after], axis=0)
    else:
        around = normed
    q = dot(normed, w["q"]()).astype(jnp.bfloat16) * jnp.bfloat16(0.125)
    k = dot(around, w["k"]()).astype(jnp.bfloat16)
    v = dot(around, w["v"]()).astype(jnp.bfloat16)
    first_lane = lax.broadcasted_iota(jnp.int32, (HALFROWS, 128), 1) < 64
    ones = jnp.ones((OWN, 128), jnp.bfloat16)
    for half in range(2):
        bias = half_bias(shifted, half, edge_ref[0], edge_ref[1])
        bias = jnp.concatenate([bias, bias], axis=0)
        for micro in range(count):
            top = micro * OWN + half * HALFROWS
            rows = slice(top, top + HALFROWS)
            start = half * OWN if shifted else micro * OWN
            keys = slice(start, start + OWN)
            for pair in range(4):
                cols = slice(pair * 128, (pair + 1) * 128)
                mixed_ref[rows, cols] = attention(
                    q[rows, cols], k[keys, cols], v[keys, cols], bias, first_lane, ones
                )
    residual = own + dot(mixed_ref[...], w["proj"]())
    inner = layer_norm(residual, gain_ref[1:2, :]).astype(jnp.bfloat16)
    total = residual
    for t in range(4):
        hidden = jax.nn.gelu(dot(inner, w["up%d" % t]())).astype(jnp.bfloat16)
        down = jnp.concatenate([tiles[8 + u, 8 * t + j] for j in range(8) for u in range(4)], axis=0)
        total = total + dot(hidden, down)
    result = total.astype(jnp.bfloat16)
    outs["out"][...] = result.reshape(count, OWN, D)
    if joins:
        result = (result.astype(jnp.float32) + load("skip")).astype(jnp.bfloat16)
        outs["joined"][...] = result.reshape(count, OWN, D)
    if not shifted:
        whole = result.reshape(count, OWN, D)
        outs["top"][...] = whole[:, :HALFROWS]
        outs["bottom"][...] = whole[:, HALFROWS:]


ZS, YS = 8, 4
LATS = 2 * ZS * YS
PAIRS = [(0, 3), (1, 2)]


def run_block(weights, own, gains, edges, count=1, halo=None, skip=None):
    shifted = halo is not None
    joins = skip is not None
    operands = {"own": own}
    if shifted:
        operands["prev"], operands["next"] = halo
    if joins:
        operands["skip"] = skip
    names = list(operands)
    rows = {"out": OWN}
    if joins:
        rows["joined"] = OWN
    if not shifted:
        rows["top"] = rows["bottom"] = HALFROWS

    def body(edge_ref, gain_ref, tiles, *rest):
        refs = {name: (rest[i], operands[name][1]) for i, name in enumerate(names)}
        outs = dict(zip(rows, rest[len(names) :]))
        block_kernel(shifted, joins, count, edge_ref, refs, gain_ref, tiles, outs, rest[-1])

    vmem = pl.BlockSpec(memory_space=pltpu.VMEM)
    results = pl.pallas_call(
        body,
        out_shape=tuple(jax.ShapeDtypeStruct((count, n, D), jnp.bfloat16) for n in rows.values()),
        in_specs=[pl.BlockSpec(memory_space=pltpu.SMEM), vmem, vmem] + [vmem] * len(names),
        out_specs=(vmem,) * len(rows),
        scratch_shapes=[pltpu.VMEM((count * OWN, D), jnp.bfloat16)],
        compiler_params=pltpu.CompilerParams(vmem_limit_bytes=28 * 1024 * 1024),
        cost_estimate=pl.CostEstimate(flops=count * 5 * 10**9, bytes_accessed=7 * 10**6, transcendentals=10**6),
    )(edges, gains, pltpu.with_memory_space_constraint(weights, pltpu.VMEM), *(operands[name][0] for name in names))
    return dict(zip(rows, results))


def pack(w_qkv, w_proj, w_up, w_down):
    def body(qkv, proj, up, down, out):
        wide = [qkv[...].astype(jnp.float32), proj[...].astype(jnp.float32), up[...].astype(jnp.float32)]
        parts = [wide[0][:, i * D : (i + 1) * D] for i in range(3)] + [wide[1]]
        parts += [wide[2][:, i * D : (i + 1) * D] for i in range(4)] + [down[...].astype(jnp.float32)]
        out[...] = jnp.concatenate(parts, axis=0).astype(jnp.bfloat16)

    vmem = pl.BlockSpec(memory_space=pltpu.VMEM)
    return pl.pallas_call(
        body,
        out_shape=jax.ShapeDtypeStruct((96, D), jnp.bfloat16),
        in_specs=[vmem] * 4,
        out_specs=vmem,
    )(w_qkv, w_proj, w_up, w_down)


def assemble(place, mine, passed, last_step):
    def body(place_ref, *rest):
        out = rest[16]
        z0, y0, core = place_ref[0], place_ref[1], place_ref[2]
        for side in range(2):
            source_core = core if side == 0 else 1 - core
            base = 6 * source_core
            for line, inners in enumerate(((0, -1), (1, last_step))):
                for piece, outer in enumerate((0, -1, 1, (-2, 2)[line])):
                    ref = rest[8 * side + 4 * line + piece]
                    for n, inner in enumerate(inners):
                        for far in range(2):
                            z_step = jnp.where(source_core == 0, inner, outer) + 4 * far
                            y_step = jnp.where(source_core == 0, outer, inner)
                            chip = lax.rem(z0 + z_step + ZS, ZS) * YS + lax.rem(y0 + y_step + YS, YS)
                            for tile in range(6):
                                out[base + tile, chip] = ref[n, far, tile]

    vmem = pl.BlockSpec(memory_space=pltpu.VMEM)
    return pl.pallas_call(
        body,
        out_shape=pltpu.VMEM((12, 32, 16, D), jnp.bfloat16),
        in_specs=[pl.BlockSpec(memory_space=pltpu.SMEM)] + [vmem] * 16,
        out_specs=vmem,
        compiler_params=pltpu.CompilerParams(vmem_limit_bytes=24 * 1024 * 1024),
        cost_estimate=pl.CostEstimate(flops=10**9, bytes_accessed=6 * 10**6, transcendentals=0),
    )(place, *mine, *passed)


def lat_id(z, y, core):
    return ((z % ZS) * YS + y % YS) * 2 + core


def moved(along):
    pairs = []
    for z in range(ZS):
        for y in range(YS):
            for core in range(2):
                dz, dy = along(core)
                pairs.append((lat_id(z, y, core), lat_id(z + dz, y + dy, core)))
    return pairs


def ring(level, step):
    return moved(lambda core: (step, 0) if (level == 0) == (core == 0) else (0, step))


SWAP = [(i, i ^ 1) for i in range(LATS)]


def send(value, pairs):
    return lax.ppermute(value, "lat", pairs)


def second_ring_start(lines):
    return [[line, send(line, ring(1, 1)), send(line, ring(1, -1))] for line in lines]


def second_ring_end(place, parts, last_step):
    near, far = parts
    mine = near + [send(near[1], ring(1, 1))] + far + [send(far[2], ring(1, -1))]
    return assemble(place, mine, [send(piece, SWAP) for piece in mine], last_step)


def gather_weights(place, even, shard):
    both = jnp.stack([shard, send(shard, moved(lambda core: (4, 0)))])
    other = lax.ppermute(both, "segment", [(0, 1), (1, 0), (2, 3), (3, 2)])
    base = jnp.stack([jnp.where(even, both, other), jnp.where(even, other, both)])
    before, after = send(base, ring(0, 1)), send(base, ring(0, -1))
    far = [send(before[0], ring(0, 1)), send(after[1], ring(0, -1))]
    lines = [(jnp.stack([base[b], before[b]]), jnp.stack([after[b], far[b]])) for b in range(2)]
    first = second_ring_start(lines[0])
    first, line = lax.optimization_barrier((first, lines[1]))
    second = second_ring_start(line)
    return second_ring_end(place, first, -2), second_ring_end(place, second, 2)


def on_device(tokens, norm_gain, w_qkv, w_proj, w_up, w_down):
    segment = lax.axis_index("segment")
    lat = lax.axis_index("lat")
    core = lat % 2
    even = segment % 2 == 0
    low = (segment == 0) | (segment == 3)
    place = jnp.stack([lat // (2 * YS), (lat // 2) % YS, core]).astype(jnp.int32)
    edges = jnp.stack([lat > 0, lat < LATS - 1]).astype(jnp.int32)

    own = pack(w_qkv[0], w_proj[0], w_up[0], w_down[0])
    other = send(own, SWAP)
    first, second = jnp.where(core == 0, own, other), jnp.where(core == 0, other, own)
    tall = jnp.stack([first[:64].reshape(8, 8, D), second[:64].reshape(8, 8, D)], axis=1).reshape(8, 16, D)
    tall = jnp.concatenate([tall, first[64:].reshape(2, 16, D), second[64:].reshape(2, 16, D)], axis=0)
    shard = jnp.where(core == 0, tall[:6], tall[6:])
    weights = gather_weights(place, even, shard)
    other_gain = lax.ppermute(norm_gain[0], "segment", [(0, 1), (1, 0), (2, 3), (3, 2)])
    gains = [jnp.where(even, norm_gain[0], other_gain), jnp.where(even, other_gain, norm_gain[0])]

    fields = jnp.where(low, tokens[:2], tokens[2:])
    fields = fields.reshape(2, LEVELS, 2, 6, 6, D).transpose(0, 2, 1, 3, 4, 5).reshape(2, OWN, D)

    def halo(block):
        up = send(block["bottom"], [(i, i + 1) for i in range(LATS - 1)])
        down = send(block["top"], [(i + 1, i) for i in range(LATS - 1)])
        return up, down

    def pass_on(value, pairs):
        return lax.ppermute(value, "segment", pairs)

    pair = range(2)
    e0 = run_block(weights[0], (fields, None), gains[0], edges, count=2)
    a0 = e0["out"]
    around = halo(e0)
    a1 = [
        run_block(weights[1], (a0, m), gains[1], edges, halo=[(side, m) for side in around])["out"] for m in pair
    ]
    skip = pass_on(a0, PAIRS)
    entering = [pass_on(a1[m], PAIRS) for m in pair]
    e1 = [run_block(weights[0], (entering[m], 0), gains[0], edges, skip=(skip, m)) for m in pair]
    a2 = [block["out"] for block in e1]
    a3 = [
        run_block(weights[1], (block["joined"], 0), gains[1], edges, halo=[(side, 0) for side in halo(block)])["out"]
        for block in e1
    ]

    down_out = pass_on(jnp.where(segment == 1, a0, jnp.concatenate(a1, axis=0)), [(0, 1), (1, 0)])
    up_out = [pass_on(jnp.where(segment == 3, a2[m], a3[m]), [(2, 3), (3, 2)]) for m in pair]

    kept, got = [], []
    for m in pair:
        first_stage = jnp.where(segment == 0, a0[m : m + 1], a1[m])
        second_stage = jnp.where(segment == 2, a2[m], a3[m])
        kept.append(jnp.where(segment < 2, first_stage, second_stage))
        got.append(jnp.where(segment < 2, down_out[m : m + 1], up_out[m]))
    outs = [jnp.where(low, kept[m], got[m]) for m in pair] + [jnp.where(low, got[m], kept[m]) for m in pair]
    out = jnp.concatenate(outs, axis=0).reshape(4, 2, LEVELS, 6, 6, D).transpose(0, 2, 1, 3, 4, 5)
    return out.reshape(1, 4, LEVELS, 12, 6, D)


def solution(mesh):
    return jax.shard_map(
        on_device,
        mesh=mesh,
        in_specs=(
            P(None, None, "lat", None, None),
            P("segment", None, None),
            P("segment", "lat", None),
            P("segment", "lat", None),
            P("segment", "lat", None),
            P("segment", "lat", None),
        ),
        out_specs=P("segment", None, None, "lat", None, None),
        check_vma=False,
    )
```

```python
import jax
import jax.numpy as jnp
from jax import lax
from jax.experimental import pallas as pl
from jax.experimental.pallas import tpu as pltpu
from jax.sharding import PartitionSpec as P

D = 512
LEVELS = 4
HALFROWS = 144
OWN = 288
PER_LEVEL = 36
EPS = 1e-5


def layer_norm(wide, gain):
    center = jnp.mean(wide, axis=-1, keepdims=True)
    moved = wide - center
    spread = jnp.mean(moved * moved, axis=-1, keepdims=True)
    return moved * lax.rsqrt(spread + EPS) * gain


def dot(a, b):
    return jnp.dot(a, b, preferred_element_type=jnp.float32)


def attention(q, k, v, bias, first_lane, ones):
    zero = jnp.zeros_like(q)
    stacked = jnp.concatenate([jnp.where(first_lane, q, zero), jnp.where(first_lane, zero, q)], axis=0)
    scores = lax.dot_general(stacked, k, (((1,), (1,)), ((), ())), preferred_element_type=jnp.float32)
    scores = scores + bias
    top = jnp.max(scores, axis=-1, keepdims=True)
    terms = jnp.exp(scores - top).astype(jnp.bfloat16)
    both = dot(terms, jnp.concatenate([v, ones], axis=1))
    rows = q.shape[0]
    weighed = jnp.where(first_lane, both[:rows, :128], both[rows:, :128])
    total = jnp.where(first_lane, both[:rows, 128:], both[rows:, 128:])
    return (weighed / total).astype(jnp.bfloat16)


def half_bias(shifted, half, has_prev, has_next):
    row = lax.broadcasted_iota(jnp.int32, (HALFROWS, OWN), 0)
    col = lax.broadcasted_iota(jnp.int32, (HALFROWS, OWN), 1)
    far = col >= HALFROWS
    key = jnp.where(far, col - HALFROWS, col)

    def level(i):
        return ((i >= PER_LEVEL).astype(jnp.int32) + (i >= 2 * PER_LEVEL).astype(jnp.int32)
                + (i >= 3 * PER_LEVEL).astype(jnp.int32))

    row_level, key_level = level(row), level(key)
    if shifted:
        group = lambda l: jnp.where(l == 2, 1, l)
        allowed = group(row_level) == group(key_level)
        if half == 0:
            allowed = allowed & (far | (has_prev > 0))
        else:
            allowed = allowed & (jnp.logical_not(far) | (has_next > 0))
    else:
        group = lambda l: (l >= 2).astype(jnp.int32)
        allowed = group(row_level) == group(key_level)
    return jnp.where(allowed, 0.0, -1e30).astype(jnp.float32)


def block_kernel(shifted, joins, count, parts, edge_ref, refs, gain_ref, tiles, outs, mixed_ref):
    names = ("q", "k", "v", "proj", "up0", "up1", "up2", "up3")
    w = {name: (lambda i=i: tiles[i].reshape(D, D)) for i, name in enumerate(names)}

    def load(name):
        ref, index = refs[name]
        if index is None:
            return ref[...].reshape(-1, D).astype(jnp.float32)
        return ref[index].astype(jnp.float32)

    own = jnp.concatenate([load("own%d" % i) for i in range(parts)], axis=0)
    gain0 = gain_ref[0:1, :]
    normed = layer_norm(own, gain0).astype(jnp.bfloat16)
    if shifted:
        before = layer_norm(load("prev"), gain0).astype(jnp.bfloat16)
        after = layer_norm(load("next"), gain0).astype(jnp.bfloat16)
        around = jnp.concatenate([before, normed, after], axis=0)
    else:
        around = normed
    q = dot(normed, w["q"]()).astype(jnp.bfloat16) * jnp.bfloat16(0.125)
    k = dot(around, w["k"]()).astype(jnp.bfloat16)
    v = dot(around, w["v"]()).astype(jnp.bfloat16)
    first_lane = lax.broadcasted_iota(jnp.int32, (HALFROWS, 128), 1) < 64
    ones = jnp.ones((OWN, 128), jnp.bfloat16)
    for half in range(2):
        bias = half_bias(shifted, half, edge_ref[0], edge_ref[1])
        bias = jnp.concatenate([bias, bias], axis=0)
        for micro in range(count):
            top = micro * OWN + half * HALFROWS
            rows = slice(top, top + HALFROWS)
            start = half * OWN if shifted else micro * OWN
            keys = slice(start, start + OWN)
            for pair in range(4):
                cols = slice(pair * 128, (pair + 1) * 128)
                mixed_ref[rows, cols] = attention(
                    q[rows, cols], k[keys, cols], v[keys, cols], bias, first_lane, ones
                )
    residual = own + dot(mixed_ref[...], w["proj"]())
    inner = layer_norm(residual, gain_ref[1:2, :]).astype(jnp.bfloat16)
    total = residual
    for t in range(4):
        hidden = jax.nn.gelu(dot(inner, w["up%d" % t]())).astype(jnp.bfloat16)
        down = jnp.concatenate([tiles[8 + u, 8 * t + j] for j in range(8) for u in range(4)], axis=0)
        total = total + dot(hidden, down)
    result = total.astype(jnp.bfloat16)
    outs["out"][...] = result.reshape(count, OWN, D)
    if joins:
        result = (result.astype(jnp.float32) + load("skip")).astype(jnp.bfloat16)
        outs["joined"][...] = result.reshape(count, OWN, D)
    if not shifted:
        whole = result.reshape(count, OWN, D)
        outs["top"][...] = whole[:, :HALFROWS]
        outs["bottom"][...] = whole[:, HALFROWS:]


ZS, YS = 8, 4
LATS = 2 * ZS * YS
PAIRS = [(0, 3), (1, 2)]


def run_block(weights, own, gains, edges, halo=None, skip=None):
    shifted = halo is not None
    joins = skip is not None
    operands = {"own%d" % i: field for i, field in enumerate(own)}
    count = sum(1 if index is not None else array.shape[0] for array, index in own)
    if shifted:
        operands["prev"], operands["next"] = halo
    if joins:
        operands["skip"] = skip
    names = list(operands)
    rows = {"out": OWN}
    if joins:
        rows["joined"] = OWN
    if not shifted:
        rows["top"] = rows["bottom"] = HALFROWS

    def body(edge_ref, gain_ref, tiles, *rest):
        refs = {name: (rest[i], operands[name][1]) for i, name in enumerate(names)}
        outs = dict(zip(rows, rest[len(names) :]))
        block_kernel(shifted, joins, count, len(own), edge_ref, refs, gain_ref, tiles, outs, rest[-1])

    vmem = pl.BlockSpec(memory_space=pltpu.VMEM)
    results = pl.pallas_call(
        body,
        out_shape=tuple(jax.ShapeDtypeStruct((count, n, D), jnp.bfloat16) for n in rows.values()),
        in_specs=[pl.BlockSpec(memory_space=pltpu.SMEM), vmem, vmem] + [vmem] * len(names),
        out_specs=(vmem,) * len(rows),
        scratch_shapes=[pltpu.VMEM((count * OWN, D), jnp.bfloat16)],
        compiler_params=pltpu.CompilerParams(vmem_limit_bytes=(10 + 6 * count) * 1024 * 1024),
        cost_estimate=pl.CostEstimate(flops=count * 5 * 10**9, bytes_accessed=7 * 10**6, transcendentals=10**6),
    )(edges, gains, pltpu.with_memory_space_constraint(weights, pltpu.VMEM), *(operands[name][0] for name in names))
    return dict(zip(rows, results))


def pack(w_qkv, w_proj, w_up, w_down):
    def body(qkv, proj, up, down, out):
        wide = [qkv[...].astype(jnp.float32), proj[...].astype(jnp.float32), up[...].astype(jnp.float32)]
        parts = [wide[0][:, i * D : (i + 1) * D] for i in range(3)] + [wide[1]]
        parts += [wide[2][:, i * D : (i + 1) * D] for i in range(4)] + [down[...].astype(jnp.float32)]
        out[...] = jnp.concatenate(parts, axis=0).astype(jnp.bfloat16)

    vmem = pl.BlockSpec(memory_space=pltpu.VMEM)
    return pl.pallas_call(
        body,
        out_shape=jax.ShapeDtypeStruct((96, D), jnp.bfloat16),
        in_specs=[vmem] * 4,
        out_specs=vmem,
    )(w_qkv, w_proj, w_up, w_down)


def assemble(place, mine, passed, last_step):
    def body(place_ref, *rest):
        out, sems = rest[16], rest[17]
        z0, y0, core = place_ref[0], place_ref[1], place_ref[2]
        copies = []
        for side in range(2):
            source_core = core if side == 0 else 1 - core
            base = 6 * source_core
            for line, inners in enumerate(((0, -1), (1, last_step))):
                for piece, outer in enumerate((0, -1, 1, (-2, 2)[line])):
                    ref = rest[8 * side + 4 * line + piece]
                    for n, inner in enumerate(inners):
                        for far in range(2):
                            z_step = jnp.where(source_core == 0, inner, outer) + 4 * far
                            y_step = jnp.where(source_core == 0, outer, inner)
                            chip = lax.rem(z0 + z_step + ZS, ZS) * YS + lax.rem(y0 + y_step + YS, YS)
                            copy = pltpu.make_async_copy(
                                ref.at[n, far], out.at[pl.ds(base, 6), chip], sems.at[len(copies)]
                            )
                            copy.start()
                            copies.append(copy)
        for copy in copies:
            copy.wait()

    return pl.pallas_call(
        body,
        out_shape=pltpu.VMEM((12, 32, 16, D), jnp.bfloat16),
        in_specs=[pl.BlockSpec(memory_space=pltpu.SMEM)] + [pl.BlockSpec(memory_space=pl.ANY)] * 16,
        out_specs=pl.BlockSpec(memory_space=pltpu.VMEM),
        scratch_shapes=[pltpu.SemaphoreType.DMA((64,))],
        compiler_params=pltpu.CompilerParams(vmem_limit_bytes=16 * 1024 * 1024),
        cost_estimate=pl.CostEstimate(flops=10**9, bytes_accessed=6 * 10**6, transcendentals=0),
    )(place, *(pltpu.with_memory_space_constraint(piece, pltpu.HBM) for piece in (*mine, *passed)))


def lat_id(z, y, core):
    return ((z % ZS) * YS + y % YS) * 2 + core


def moved(along):
    pairs = []
    for z in range(ZS):
        for y in range(YS):
            for core in range(2):
                dz, dy = along(core)
                pairs.append((lat_id(z, y, core), lat_id(z + dz, y + dy, core)))
    return pairs


def ring(level, step):
    return moved(lambda core: (step, 0) if (level == 0) == (core == 0) else (0, step))


SWAP = [(i, i ^ 1) for i in range(LATS)]


def send(value, pairs):
    return lax.ppermute(value, "lat", pairs)


def second_ring(first, second):
    near = [first, send(first, ring(1, 1)), send(first, ring(1, -1))]
    distant = [second, send(second, ring(1, 1)), send(second, ring(1, -1))]
    mine = near + [send(near[1], ring(1, 1))] + distant + [send(distant[2], ring(1, -1))]
    return mine, [send(piece, SWAP) for piece in mine]


def gather_weights(place, even, shard, early):
    both = jnp.stack([shard, send(shard, moved(lambda core: (4, 0)))])
    both, early = lax.optimization_barrier((both, early))
    other = lax.ppermute(both, "segment", [(0, 1), (1, 0), (2, 3), (3, 2)])
    base = jnp.stack([jnp.where(even, both, other), jnp.where(even, other, both)])
    before, after = send(base, ring(0, 1)), send(base, ring(0, -1))
    far = lax.optimization_barrier((send(before[0], ring(0, 1)), send(after[1], ring(0, -1))))
    lines = [(jnp.stack([base[b], before[b]]), jnp.stack([after[b], far[b]])) for b in range(2)]
    first = second_ring(*lines[0])
    first, line = lax.optimization_barrier((first, lines[1]))
    second = second_ring(*line)
    return [assemble(place, *first, -2), assemble(place, *second, 2)], early


def on_device(tokens, norm_gain, w_qkv, w_proj, w_up, w_down):
    segment = lax.axis_index("segment")
    lat = lax.axis_index("lat")
    core = lat % 2
    even = segment % 2 == 0
    low = (segment == 0) | (segment == 3)
    place = jnp.stack([lat // (2 * YS), (lat // 2) % YS, core]).astype(jnp.int32)
    edges = jnp.stack([lat > 0, lat < LATS - 1]).astype(jnp.int32)

    own = pack(w_qkv[0], w_proj[0], w_up[0], w_down[0])
    other = send(own, SWAP)
    first, second = jnp.where(core == 0, own, other), jnp.where(core == 0, other, own)
    tall = jnp.stack([first[:64].reshape(8, 8, D), second[:64].reshape(8, 8, D)], axis=1).reshape(8, 16, D)
    tall = jnp.concatenate([tall, first[64:].reshape(2, 16, D), second[64:].reshape(2, 16, D)], axis=0)
    shard = jnp.where(core == 0, tall[:6], tall[6:])
    other_gain = lax.ppermute(norm_gain[0], "segment", [(0, 1), (1, 0), (2, 3), (3, 2)])
    fields = jnp.where(low, tokens[:2], tokens[2:])
    fields = fields.reshape(2, LEVELS, 2, 6, 6, D).transpose(0, 2, 1, 3, 4, 5).reshape(2, OWN, D)
    weights, (other_gain, fields) = gather_weights(place, even, shard, (other_gain, fields))
    gains = [jnp.where(even, norm_gain[0], other_gain), jnp.where(even, other_gain, norm_gain[0])]

    def halo(block):
        up = send(block["bottom"], [(i, i + 1) for i in range(LATS - 1)])
        down = send(block["top"], [(i + 1, i) for i in range(LATS - 1)])
        return up, down

    def pass_on(value, pairs):
        return lax.ppermute(value, "segment", pairs)

    pair = range(2)
    e0 = run_block(weights[0], [(fields, None)], gains[0], edges)
    a0 = e0["out"]
    around = halo(e0)
    a1 = [
        run_block(weights[1], [(a0, m)], gains[1], edges, halo=[(side, m) for side in around])["out"] for m in pair
    ]
    skip = pass_on(a0, PAIRS)
    entering = [(pass_on(a1[m], PAIRS), None) for m in pair]
    e1 = run_block(weights[0], entering, gains[0], edges, skip=(skip, None))
    a2 = e1["out"]
    around = halo(e1)
    a3 = [
        run_block(weights[1], [(e1["joined"], m)], gains[1], edges, halo=[(side, m) for side in around])["out"]
        for m in pair
    ]

    down_out = pass_on(jnp.where(segment == 1, a0, jnp.concatenate(a1, axis=0)), [(0, 1), (1, 0)])
    up_out = [pass_on(jnp.where(segment == 3, a2[m : m + 1], a3[m]), [(2, 3), (3, 2)]) for m in pair]

    out = jnp.zeros((1, 4, LEVELS, 12, 6, D), jnp.bfloat16)

    def place_out(out, field, slot):
        field = field.reshape(1, 1, 2, LEVELS, 6, 6, D).transpose(0, 1, 3, 2, 4, 5, 6).reshape(1, 1, LEVELS, 12, 6, D)
        return lax.dynamic_update_slice(out, field, (0, slot, 0, 0, 0, 0))

    for m in pair:
        first_stage = jnp.where(segment == 0, a0[m : m + 1], a1[m])
        second_stage = jnp.where(segment == 2, a2[m : m + 1], a3[m])
        kept = jnp.where(segment < 2, first_stage, second_stage)
        out = place_out(out, kept, jnp.where(low, m, m + 2))
        got = jnp.where(segment < 2, down_out[m : m + 1], up_out[m])
        out = place_out(out, got, jnp.where(low, m + 2, m))
    return out


def solution(mesh):
    return jax.shard_map(
        on_device,
        mesh=mesh,
        in_specs=(
            P(None, None, "lat", None, None),
            P("segment", None, None),
            P("segment", "lat", None),
            P("segment", "lat", None),
            P("segment", "lat", None),
            P("segment", "lat", None),
        ),
        out_specs=P("segment", None, None, "lat", None, None),
        check_vma=False,
    )
```

```python
import jax
import jax.numpy as jnp
from jax import lax
from jax.experimental import pallas as pl
from jax.experimental.pallas import tpu as pltpu
from jax.sharding import PartitionSpec as P

D = 512
LEVELS = 4
HALFROWS = 144
OWN = 288
PER_LEVEL = 36
EPS = 1e-5


def layer_norm(wide, gain):
    center = jnp.mean(wide, axis=-1, keepdims=True)
    moved = wide - center
    spread = jnp.mean(moved * moved, axis=-1, keepdims=True)
    return moved * lax.rsqrt(spread + EPS) * gain


def dot(a, b):
    return jnp.dot(a, b, preferred_element_type=jnp.float32)


def attention(q, k, v, bias):
    rows, keys = q.shape[0], k.shape[0]
    first_lane = lax.broadcasted_iota(jnp.int32, (rows, 128), 1) < 64
    zero = jnp.zeros_like(q)
    stacked = jnp.concatenate([jnp.where(first_lane, q, zero), jnp.where(first_lane, zero, q)], axis=0)
    stacked = stacked.astype(jnp.bfloat16)
    k, v = k.astype(jnp.bfloat16), v.astype(jnp.bfloat16)
    scores = lax.dot_general(stacked, k, (((1,), (1,)), ((), ())), preferred_element_type=jnp.float32)
    if bias is not None:
        scores = scores + bias
    top = jnp.max(scores, axis=-1, keepdims=True)
    terms = jnp.exp(scores - top).astype(jnp.bfloat16)
    both = dot(terms, jnp.concatenate([v, jnp.ones((keys, 128), jnp.bfloat16)], axis=1))
    weighed = jnp.where(first_lane, both[:rows, :128], both[rows:, :128])
    total = jnp.where(first_lane, both[:rows, 128:], both[rows:, 128:])
    return weighed / total


GROUP = 72


def group_bias(split, half, has_prev, has_next):
    row = lax.broadcasted_iota(jnp.int32, (2 * GROUP, 2 * GROUP), 0)
    col = lax.broadcasted_iota(jnp.int32, (2 * GROUP, 2 * GROUP), 1)
    far = col >= GROUP
    valid = (far | (has_prev > 0)) if half == 0 else (jnp.logical_not(far) | (has_next > 0))
    if split:
        query = jnp.where(row >= GROUP, row - GROUP, row) >= PER_LEVEL
        key = jnp.where(far, col - GROUP, col) >= PER_LEVEL
        valid = valid & (query == key)
    return jnp.where(valid, 0.0, -1e30).astype(jnp.float32)


def pairs_together(x):
    parts = [x[i : i + GROUP] for i in range(0, x.shape[0], GROUP)]
    return jnp.concatenate([parts[4 * (i // 4) + (0, 2, 1, 3)[i % 4]] for i in range(len(parts))], axis=0)


def turned(x, steps):
    halves = [x[i : i + HALFROWS] for i in range(0, x.shape[0], HALFROWS)]
    return jnp.concatenate([pltpu.roll(half, (steps * PER_LEVEL) % HALFROWS, 0) for half in halves], axis=0)


def block_kernel(shifted, joins, count, parts, edge_ref, refs, gain_ref, tiles, outs, mixed_ref):
    names = ("q", "k", "v", "proj", "up0", "up1", "up2", "up3")
    w = {name: (lambda i=i: tiles[i].reshape(D, D)) for i, name in enumerate(names)}

    def load(name):
        ref, index = refs[name]
        if index is None:
            return ref[...].reshape(-1, D).astype(jnp.float32)
        return ref[index].astype(jnp.float32)

    own = jnp.concatenate([load("own%d" % i) for i in range(parts)], axis=0)
    own = turned(own, -1) if shifted else pairs_together(own)
    gain0 = gain_ref[0:1, :]
    normed = layer_norm(own, gain0).astype(jnp.bfloat16)
    if shifted:
        before = layer_norm(turned(load("prev"), -1), gain0).astype(jnp.bfloat16)
        after = layer_norm(turned(load("next"), -1), gain0).astype(jnp.bfloat16)
        around = jnp.concatenate([before, normed, after], axis=0)
    else:
        around = normed
    q = dot(normed, w["q"]()) * 0.125
    k = dot(around, w["k"]())
    v = dot(around, w["v"]())
    columns = [slice(pair * 128, (pair + 1) * 128) for pair in range(4)]
    if shifted:
        for half in range(2):
            for group in range(2):
                bias = group_bias(group == 1, half, edge_ref[0], edge_ref[1])
                top = half * HALFROWS + group * GROUP
                near, far = half * OWN + group * GROUP, half * OWN + HALFROWS + group * GROUP
                for cols in columns:
                    keys, values = (
                        jnp.concatenate([x[near : near + GROUP, cols], x[far : far + GROUP, cols]], axis=0) for x in (k, v)
                    )
                    mixed_ref[top : top + GROUP, cols] = attention(q[top : top + GROUP, cols], keys, values, bias)
    else:
        for top in range(0, count * OWN, HALFROWS):
            rows = slice(top, top + HALFROWS)
            for cols in columns:
                mixed_ref[rows, cols] = attention(q[rows, cols], k[rows, cols], v[rows, cols], None)
    residual = own + dot(mixed_ref[...].astype(jnp.bfloat16), w["proj"]())
    inner = layer_norm(residual, gain_ref[1:2, :]).astype(jnp.bfloat16)
    total = residual
    for t in range(4):
        hidden = jax.nn.gelu(dot(inner, w["up%d" % t]())).astype(jnp.bfloat16)
        down = jnp.concatenate([tiles[8 + u, 8 * t + j] for j in range(8) for u in range(4)], axis=0)
        total = total + dot(hidden, down)
    result = (turned(total, 1) if shifted else pairs_together(total)).astype(jnp.bfloat16)
    outs["out"][...] = result.reshape(count, OWN, D)
    if joins:
        result = (result.astype(jnp.float32) + load("skip")).astype(jnp.bfloat16)
        outs["joined"][...] = result.reshape(count, OWN, D)
    if not shifted:
        whole = result.reshape(count, OWN, D)
        outs["top"][...] = whole[:, :HALFROWS]
        outs["bottom"][...] = whole[:, HALFROWS:]


ZS, YS = 8, 4
LATS = 2 * ZS * YS
PAIRS = [(0, 3), (1, 2)]


def run_block(weights, own, gains, edges, halo=None, skip=None):
    shifted = halo is not None
    joins = skip is not None
    operands = {"own%d" % i: field for i, field in enumerate(own)}
    count = sum(1 if index is not None else array.shape[0] for array, index in own)
    if shifted:
        operands["prev"], operands["next"] = halo
    if joins:
        operands["skip"] = skip
    names = list(operands)
    rows = {"out": OWN}
    if joins:
        rows["joined"] = OWN
    if not shifted:
        rows["top"] = rows["bottom"] = HALFROWS

    def body(edge_ref, gain_ref, tiles, *rest):
        refs = {name: (rest[i], operands[name][1]) for i, name in enumerate(names)}
        outs = dict(zip(rows, rest[len(names) :]))
        block_kernel(shifted, joins, count, len(own), edge_ref, refs, gain_ref, tiles, outs, rest[-1])

    vmem = pl.BlockSpec(memory_space=pltpu.VMEM)
    results = pl.pallas_call(
        body,
        out_shape=tuple(jax.ShapeDtypeStruct((count, n, D), jnp.bfloat16) for n in rows.values()),
        in_specs=[pl.BlockSpec(memory_space=pltpu.SMEM), vmem, vmem] + [vmem] * len(names),
        out_specs=(vmem,) * len(rows),
        scratch_shapes=[pltpu.VMEM((count * OWN, D), jnp.float32)],
        compiler_params=pltpu.CompilerParams(vmem_limit_bytes=(10 + 6 * count) * 1024 * 1024),
        cost_estimate=pl.CostEstimate(flops=count * 5 * 10**9, bytes_accessed=7 * 10**6, transcendentals=10**6),
    )(edges, gains, pltpu.with_memory_space_constraint(weights, pltpu.VMEM), *(operands[name][0] for name in names))
    return dict(zip(rows, results))


def pack(w_qkv, w_proj, w_up, w_down):
    def body(qkv, proj, up, down, out):
        wide = [qkv[...].astype(jnp.float32), proj[...].astype(jnp.float32), up[...].astype(jnp.float32)]
        parts = [wide[0][:, i * D : (i + 1) * D] for i in range(3)] + [wide[1]]
        parts += [wide[2][:, i * D : (i + 1) * D] for i in range(4)] + [down[...].astype(jnp.float32)]
        out[...] = jnp.concatenate(parts, axis=0).astype(jnp.bfloat16)

    vmem = pl.BlockSpec(memory_space=pltpu.VMEM)
    return pl.pallas_call(
        body,
        out_shape=jax.ShapeDtypeStruct((96, D), jnp.bfloat16),
        in_specs=[vmem] * 4,
        out_specs=vmem,
    )(w_qkv, w_proj, w_up, w_down)


def assemble(place, mine, passed, last_step):
    def body(place_ref, *rest):
        out, sems = rest[16], rest[17]
        z0, y0, core = place_ref[0], place_ref[1], place_ref[2]
        copies = []
        for side in range(2):
            source_core = core if side == 0 else 1 - core
            base = 6 * source_core
            for line, inners in enumerate(((0, -1), (1, last_step))):
                for piece, outer in enumerate((0, -1, 1, (-2, 2)[line])):
                    ref = rest[8 * side + 4 * line + piece]
                    for n, inner in enumerate(inners):
                        for far in range(2):
                            z_step = jnp.where(source_core == 0, inner, outer) + 4 * far
                            y_step = jnp.where(source_core == 0, outer, inner)
                            chip = lax.rem(z0 + z_step + ZS, ZS) * YS + lax.rem(y0 + y_step + YS, YS)
                            copy = pltpu.make_async_copy(
                                ref.at[n, far], out.at[pl.ds(base, 6), chip], sems.at[len(copies)]
                            )
                            copy.start()
                            copies.append(copy)
        for copy in copies:
            copy.wait()

    return pl.pallas_call(
        body,
        out_shape=pltpu.VMEM((12, 32, 16, D), jnp.bfloat16),
        in_specs=[pl.BlockSpec(memory_space=pltpu.SMEM)] + [pl.BlockSpec(memory_space=pl.ANY)] * 16,
        out_specs=pl.BlockSpec(memory_space=pltpu.VMEM),
        scratch_shapes=[pltpu.SemaphoreType.DMA((64,))],
        compiler_params=pltpu.CompilerParams(vmem_limit_bytes=16 * 1024 * 1024),
        cost_estimate=pl.CostEstimate(flops=10**9, bytes_accessed=6 * 10**6, transcendentals=0),
    )(place, *(pltpu.with_memory_space_constraint(piece, pltpu.HBM) for piece in (*mine, *passed)))


def lat_id(z, y, core):
    return ((z % ZS) * YS + y % YS) * 2 + core


def moved(along):
    pairs = []
    for z in range(ZS):
        for y in range(YS):
            for core in range(2):
                dz, dy = along(core)
                pairs.append((lat_id(z, y, core), lat_id(z + dz, y + dy, core)))
    return pairs


def ring(level, step):
    return moved(lambda core: (step, 0) if (level == 0) == (core == 0) else (0, step))


SWAP = [(i, i ^ 1) for i in range(LATS)]


def send(value, pairs):
    return lax.ppermute(value, "lat", pairs)


def second_ring(first, second):
    near = [first, send(first, ring(1, 1)), send(first, ring(1, -1))]
    distant = [second, send(second, ring(1, 1)), send(second, ring(1, -1))]
    mine = near + [send(near[1], ring(1, 1))] + distant + [send(distant[2], ring(1, -1))]
    return mine, [send(piece, SWAP) for piece in mine]


def gather_weights(place, even, shard, early):
    both = jnp.stack([shard, send(shard, moved(lambda core: (4, 0)))])
    both, early = lax.optimization_barrier((both, early))
    other = lax.ppermute(both, "segment", [(0, 1), (1, 0), (2, 3), (3, 2)])
    base = jnp.stack([jnp.where(even, both, other), jnp.where(even, other, both)])
    before, after = send(base, ring(0, 1)), send(base, ring(0, -1))
    far = lax.optimization_barrier((send(before[0], ring(0, 1)), send(after[1], ring(0, -1))))
    lines = [(jnp.stack([base[b], before[b]]), jnp.stack([after[b], far[b]])) for b in range(2)]
    first = second_ring(*lines[0])
    first, line = lax.optimization_barrier((first, lines[1]))
    second = second_ring(*line)
    return [assemble(place, *first, -2), assemble(place, *second, 2)], early


def on_device(tokens, norm_gain, w_qkv, w_proj, w_up, w_down):
    segment = lax.axis_index("segment")
    lat = lax.axis_index("lat")
    core = lat % 2
    even = segment % 2 == 0
    low = (segment == 0) | (segment == 3)
    place = jnp.stack([lat // (2 * YS), (lat // 2) % YS, core]).astype(jnp.int32)
    edges = jnp.stack([lat > 0, lat < LATS - 1]).astype(jnp.int32)

    own = pack(w_qkv[0], w_proj[0], w_up[0], w_down[0])
    other = send(own, SWAP)
    first, second = jnp.where(core == 0, own, other), jnp.where(core == 0, other, own)
    tall = jnp.stack([first[:64].reshape(8, 8, D), second[:64].reshape(8, 8, D)], axis=1).reshape(8, 16, D)
    tall = jnp.concatenate([tall, first[64:].reshape(2, 16, D), second[64:].reshape(2, 16, D)], axis=0)
    shard = jnp.where(core == 0, tall[:6], tall[6:])
    other_gain = lax.ppermute(norm_gain[0], "segment", [(0, 1), (1, 0), (2, 3), (3, 2)])
    fields = jnp.where(low, tokens[:2], tokens[2:])
    fields = fields.reshape(2, LEVELS, 2, 6, 6, D).transpose(0, 2, 1, 3, 4, 5).reshape(2, OWN, D)
    weights, (other_gain, fields) = gather_weights(place, even, shard, (other_gain, fields))
    gains = [jnp.where(even, norm_gain[0], other_gain), jnp.where(even, other_gain, norm_gain[0])]

    def halo(block):
        up = send(block["bottom"], [(i, i + 1) for i in range(LATS - 1)])
        down = send(block["top"], [(i + 1, i) for i in range(LATS - 1)])
        return up, down

    def pass_on(value, pairs):
        return lax.ppermute(value, "segment", pairs)

    pair = range(2)
    e0 = run_block(weights[0], [(fields, None)], gains[0], edges)
    a0 = e0["out"]
    around = halo(e0)
    a1 = [
        run_block(weights[1], [(a0, m)], gains[1], edges, halo=[(side, m) for side in around])["out"] for m in pair
    ]
    skip = pass_on(a0, PAIRS)
    entering = [(pass_on(a1[m], PAIRS), None) for m in pair]
    e1 = run_block(weights[0], entering, gains[0], edges, skip=(skip, None))
    a2 = e1["out"]
    around = halo(e1)
    a3 = [
        run_block(weights[1], [(e1["joined"], m)], gains[1], edges, halo=[(side, m) for side in around])["out"]
        for m in pair
    ]

    down_out = pass_on(jnp.where(segment == 1, a0, jnp.concatenate(a1, axis=0)), [(0, 1), (1, 0)])
    up_out = [pass_on(jnp.where(segment == 3, a2[m : m + 1], a3[m]), [(2, 3), (3, 2)]) for m in pair]

    out = jnp.zeros((1, 4, LEVELS, 12, 6, D), jnp.bfloat16)

    def place_out(out, field, slot):
        field = field.reshape(1, 1, 2, LEVELS, 6, 6, D).transpose(0, 1, 3, 2, 4, 5, 6).reshape(1, 1, LEVELS, 12, 6, D)
        return lax.dynamic_update_slice(out, field, (0, slot, 0, 0, 0, 0))

    for m in pair:
        first_stage = jnp.where(segment == 0, a0[m : m + 1], a1[m])
        second_stage = jnp.where(segment == 2, a2[m : m + 1], a3[m])
        kept = jnp.where(segment < 2, first_stage, second_stage)
        out = place_out(out, kept, jnp.where(low, m, m + 2))
        got = jnp.where(segment < 2, down_out[m : m + 1], up_out[m])
        out = place_out(out, got, jnp.where(low, m + 2, m))
    return out


def solution(mesh):
    return jax.shard_map(
        on_device,
        mesh=mesh,
        in_specs=(
            P(None, None, "lat", None, None),
            P("segment", None, None),
            P("segment", "lat", None),
            P("segment", "lat", None),
            P("segment", "lat", None),
            P("segment", "lat", None),
        ),
        out_specs=P("segment", None, None, "lat", None, None),
        check_vma=False,
    )
```

```python
import jax
import jax.numpy as jnp
from jax import lax
from jax.experimental import pallas as pl
from jax.experimental.pallas import tpu as pltpu
from jax.sharding import PartitionSpec as P

D = 512
LEVELS = 4
HALFROWS = 144
OWN = 288
PER_LEVEL = 36
EPS = 1e-5


def layer_norm(wide, gain):
    center = jnp.mean(wide, axis=-1, keepdims=True)
    moved = wide - center
    spread = jnp.mean(moved * moved, axis=-1, keepdims=True)
    return moved * lax.rsqrt(spread + EPS) * gain


def dot(a, b):
    return jnp.dot(a, b, preferred_element_type=jnp.float32)


def attention(q, k, v, bias):
    rows, keys = q.shape[0], k.shape[0]
    first_lane = lax.broadcasted_iota(jnp.int32, (rows, 128), 1) < 64
    zero = jnp.zeros_like(q)
    stacked = jnp.concatenate([jnp.where(first_lane, q, zero), jnp.where(first_lane, zero, q)], axis=0)
    stacked = stacked.astype(jnp.bfloat16)
    k, v = k.astype(jnp.bfloat16), v.astype(jnp.bfloat16)
    scores = lax.dot_general(stacked, k, (((1,), (1,)), ((), ())), preferred_element_type=jnp.float32)
    if bias is not None:
        scores = scores + bias
    top = jnp.max(scores, axis=-1, keepdims=True)
    terms = jnp.exp(scores - top).astype(jnp.bfloat16)
    both = dot(terms, jnp.concatenate([v, jnp.ones((keys, 128), jnp.bfloat16)], axis=1))
    weighed = jnp.where(first_lane, both[:rows, :128], both[rows:, :128])
    total = jnp.where(first_lane, both[:rows, 128:], both[rows:, 128:])
    return weighed / total


GROUP = 72


def group_bias(split, half, has_prev, has_next):
    row = lax.broadcasted_iota(jnp.int32, (2 * GROUP, 2 * GROUP), 0)
    col = lax.broadcasted_iota(jnp.int32, (2 * GROUP, 2 * GROUP), 1)
    far = col >= GROUP
    valid = (far | (has_prev > 0)) if half == 0 else (jnp.logical_not(far) | (has_next > 0))
    if split:
        query = jnp.where(row >= GROUP, row - GROUP, row) >= PER_LEVEL
        key = jnp.where(far, col - GROUP, col) >= PER_LEVEL
        valid = valid & (query == key)
    return jnp.where(valid, 0.0, -1e30).astype(jnp.float32)


def pairs_together(x):
    parts = [x[i : i + GROUP] for i in range(0, x.shape[0], GROUP)]
    return jnp.concatenate([parts[4 * (i // 4) + (0, 2, 1, 3)[i % 4]] for i in range(len(parts))], axis=0)


def turned(x, steps):
    halves = [x[i : i + HALFROWS] for i in range(0, x.shape[0], HALFROWS)]
    return jnp.concatenate([pltpu.roll(half, (steps * PER_LEVEL) % HALFROWS, 0) for half in halves], axis=0)


def block_kernel(shifted, joins, count, parts, edge_ref, refs, gain_ref, tiles, outs, mixed_ref):
    names = ("q", "k", "v", "proj", "up0", "up1", "up2", "up3")
    w = {name: (lambda i=i: tiles[i].reshape(D, D)) for i, name in enumerate(names)}

    def load(name):
        ref, index = refs[name]
        if index is None:
            return ref[...].reshape(-1, D).astype(jnp.float32)
        return ref[index].astype(jnp.float32)

    own = jnp.concatenate([load("own%d" % i) for i in range(parts)], axis=0)
    own = turned(own, -1) if shifted else pairs_together(own)
    gain0 = gain_ref[0:1, :]
    normed = layer_norm(own, gain0).astype(jnp.bfloat16)
    if shifted:
        before = layer_norm(turned(load("prev"), -1), gain0).astype(jnp.bfloat16)
        after = layer_norm(turned(load("next"), -1), gain0).astype(jnp.bfloat16)
        around = jnp.concatenate([before, normed, after], axis=0)
    else:
        around = normed
    q = dot(normed, w["q"]()) * 0.125
    k = dot(around, w["k"]())
    v = dot(around, w["v"]())
    columns = [slice(pair * 128, (pair + 1) * 128) for pair in range(4)]
    if shifted:
        for half in range(2):
            for group in range(2):
                bias = group_bias(group == 1, half, edge_ref[0], edge_ref[1])
                top = half * HALFROWS + group * GROUP
                near, far = half * OWN + group * GROUP, half * OWN + HALFROWS + group * GROUP
                for cols in columns:
                    keys, values = (
                        jnp.concatenate([x[near : near + GROUP, cols], x[far : far + GROUP, cols]], axis=0) for x in (k, v)
                    )
                    mixed_ref[top : top + GROUP, cols] = attention(q[top : top + GROUP, cols], keys, values, bias)
    else:
        for top in range(0, count * OWN, HALFROWS):
            rows = slice(top, top + HALFROWS)
            for cols in columns:
                mixed_ref[rows, cols] = attention(q[rows, cols], k[rows, cols], v[rows, cols], None)
    residual = own + dot(mixed_ref[...].astype(jnp.bfloat16), w["proj"]())
    inner = layer_norm(residual, gain_ref[1:2, :]).astype(jnp.bfloat16)
    total = residual
    for t in range(4):
        hidden = jax.nn.gelu(dot(inner, w["up%d" % t]())).astype(jnp.bfloat16)
        down = jnp.concatenate([tiles[8 + u, 8 * t + j] for j in range(8) for u in range(4)], axis=0)
        total = total + dot(hidden, down)
    result = (turned(total, 1) if shifted else pairs_together(total)).astype(jnp.bfloat16)
    outs["out"][...] = result.reshape(count, OWN, D)
    if joins:
        result = (result.astype(jnp.float32) + load("skip")).astype(jnp.bfloat16)
        outs["joined"][...] = result.reshape(count, OWN, D)
    if not shifted:
        whole = result.reshape(count, OWN, D)
        outs["top"][...] = whole[:, :HALFROWS]
        outs["bottom"][...] = whole[:, HALFROWS:]


ZS, YS = 8, 4
LATS = 2 * ZS * YS
PAIRS = [(0, 3), (1, 2)]


def run_block(weights, own, gains, edges, halo=None, skip=None):
    shifted = halo is not None
    joins = skip is not None
    operands = {"own%d" % i: field for i, field in enumerate(own)}
    count = sum(1 if index is not None else array.shape[0] for array, index in own)
    if shifted:
        operands["prev"], operands["next"] = halo
    if joins:
        operands["skip"] = skip
    names = list(operands)
    rows = {"out": OWN}
    if joins:
        rows["joined"] = OWN
    if not shifted:
        rows["top"] = rows["bottom"] = HALFROWS

    def body(edge_ref, gain_ref, tiles, *rest):
        refs = {name: (rest[i], operands[name][1]) for i, name in enumerate(names)}
        outs = dict(zip(rows, rest[len(names) :]))
        block_kernel(shifted, joins, count, len(own), edge_ref, refs, gain_ref, tiles, outs, rest[-1])

    vmem = pl.BlockSpec(memory_space=pltpu.VMEM)
    results = pl.pallas_call(
        body,
        out_shape=tuple(jax.ShapeDtypeStruct((count, n, D), jnp.bfloat16) for n in rows.values()),
        in_specs=[pl.BlockSpec(memory_space=pltpu.SMEM), vmem, vmem] + [vmem] * len(names),
        out_specs=(vmem,) * len(rows),
        scratch_shapes=[pltpu.VMEM((count * OWN, D), jnp.float32)],
        compiler_params=pltpu.CompilerParams(vmem_limit_bytes=(10 + 6 * count) * 1024 * 1024),
        cost_estimate=pl.CostEstimate(flops=count * 5 * 10**9, bytes_accessed=7 * 10**6, transcendentals=10**6),
    )(edges, gains, pltpu.with_memory_space_constraint(weights, pltpu.VMEM), *(operands[name][0] for name in names))
    return dict(zip(rows, results))


def pack(w_qkv, w_proj, w_up, w_down):
    def body(qkv, proj, up, down, out):
        wide = [qkv[...].astype(jnp.float32), proj[...].astype(jnp.float32), up[...].astype(jnp.float32)]
        parts = [wide[0][:, i * D : (i + 1) * D] for i in range(3)] + [wide[1]]
        parts += [wide[2][:, i * D : (i + 1) * D] for i in range(4)] + [down[...].astype(jnp.float32)]
        out[...] = jnp.concatenate(parts, axis=0).astype(jnp.bfloat16)

    vmem = pl.BlockSpec(memory_space=pltpu.VMEM)
    return pl.pallas_call(
        body,
        out_shape=jax.ShapeDtypeStruct((96, D), jnp.bfloat16),
        in_specs=[vmem] * 4,
        out_specs=vmem,
    )(w_qkv, w_proj, w_up, w_down)


def assemble(place, mine, passed, last_step):
    def body(place_ref, *rest):
        out, sems = rest[16], rest[17]
        z0, y0, core = place_ref[0], place_ref[1], place_ref[2]
        copies = []
        for side in range(2):
            source_core = core if side == 0 else 1 - core
            base = 6 * source_core
            for line, inners in enumerate(((0, -1), (1, last_step))):
                for piece, outer in enumerate((0, -1, 1, (-2, 2)[line])):
                    ref = rest[8 * side + 4 * line + piece]
                    for n, inner in enumerate(inners):
                        for far in range(2):
                            z_step = jnp.where(source_core == 0, inner, outer) + 4 * far
                            y_step = jnp.where(source_core == 0, outer, inner)
                            chip = lax.rem(z0 + z_step + ZS, ZS) * YS + lax.rem(y0 + y_step + YS, YS)
                            copy = pltpu.make_async_copy(
                                ref.at[n, far], out.at[pl.ds(base, 6), chip], sems.at[len(copies)]
                            )
                            copy.start()
                            copies.append(copy)
        for copy in copies:
            copy.wait()

    pieces = [*mine, *passed]
    for i in range(16):
        if i not in (11, 15):
            pieces[i] = pltpu.with_memory_space_constraint(pieces[i], pltpu.HBM)
    return pl.pallas_call(
        body,
        out_shape=pltpu.VMEM((12, 32, 16, D), jnp.bfloat16),
        in_specs=[pl.BlockSpec(memory_space=pltpu.SMEM)] + [pl.BlockSpec(memory_space=pl.ANY)] * 16,
        out_specs=pl.BlockSpec(memory_space=pltpu.VMEM),
        scratch_shapes=[pltpu.SemaphoreType.DMA((64,))],
        compiler_params=pltpu.CompilerParams(vmem_limit_bytes=16 * 1024 * 1024),
        cost_estimate=pl.CostEstimate(flops=10**9, bytes_accessed=6 * 10**6, transcendentals=0),
    )(place, *pieces)


def lat_id(z, y, core):
    return ((z % ZS) * YS + y % YS) * 2 + core


def moved(along):
    pairs = []
    for z in range(ZS):
        for y in range(YS):
            for core in range(2):
                dz, dy = along(core)
                pairs.append((lat_id(z, y, core), lat_id(z + dz, y + dy, core)))
    return pairs


def ring(level, step):
    return moved(lambda core: (step, 0) if (level == 0) == (core == 0) else (0, step))


SWAP = [(i, i ^ 1) for i in range(LATS)]


def send(value, pairs):
    return lax.ppermute(value, "lat", pairs)


def second_ring(first, second):
    near = [first, send(first, ring(1, 1)), send(first, ring(1, -1))]
    distant = [second, send(second, ring(1, 1)), send(second, ring(1, -1))]
    mine = near + [send(near[1], ring(1, 1))] + distant + [send(distant[2], ring(1, -1))]
    return mine, [send(piece, SWAP) for piece in mine]


def gather_weights(place, even, shard, early):
    both = jnp.stack([shard, send(shard, moved(lambda core: (4, 0)))])
    both, early = lax.optimization_barrier((both, early))
    other = lax.ppermute(both, "segment", [(0, 1), (1, 0), (2, 3), (3, 2)])
    base = jnp.stack([jnp.where(even, both, other), jnp.where(even, other, both)])
    before, after = send(base, ring(0, 1)), send(base, ring(0, -1))
    far = lax.optimization_barrier((send(before[0], ring(0, 1)), send(after[1], ring(0, -1))))
    lines = [(jnp.stack([base[b], before[b]]), jnp.stack([after[b], far[b]])) for b in range(2)]
    first = second_ring(*lines[0])
    first, line = lax.optimization_barrier((first, lines[1]))
    second = second_ring(*line)
    return [assemble(place, *first, -2), assemble(place, *second, 2)], early


def on_device(tokens, norm_gain, w_qkv, w_proj, w_up, w_down):
    segment = lax.axis_index("segment")
    lat = lax.axis_index("lat")
    core = lat % 2
    even = segment % 2 == 0
    low = (segment == 0) | (segment == 3)
    place = jnp.stack([lat // (2 * YS), (lat // 2) % YS, core]).astype(jnp.int32)
    edges = jnp.stack([lat > 0, lat < LATS - 1]).astype(jnp.int32)

    own = pack(w_qkv[0], w_proj[0], w_up[0], w_down[0])
    other = send(own, SWAP)
    first, second = jnp.where(core == 0, own, other), jnp.where(core == 0, other, own)
    tall = jnp.stack([first[:64].reshape(8, 8, D), second[:64].reshape(8, 8, D)], axis=1).reshape(8, 16, D)
    tall = jnp.concatenate([tall, first[64:].reshape(2, 16, D), second[64:].reshape(2, 16, D)], axis=0)
    shard = jnp.where(core == 0, tall[:6], tall[6:])
    other_gain = lax.ppermute(norm_gain[0], "segment", [(0, 1), (1, 0), (2, 3), (3, 2)])
    fields = jnp.where(low, tokens[:2], tokens[2:])
    fields = fields.reshape(2, LEVELS, 2, 6, 6, D).transpose(0, 2, 1, 3, 4, 5).reshape(2, OWN, D)
    weights, (other_gain, fields) = gather_weights(place, even, shard, (other_gain, fields))
    gains = [jnp.where(even, norm_gain[0], other_gain), jnp.where(even, other_gain, norm_gain[0])]

    def halo(block):
        up = send(block["bottom"], [(i, i + 1) for i in range(LATS - 1)])
        down = send(block["top"], [(i + 1, i) for i in range(LATS - 1)])
        return up, down

    def pass_on(value, pairs):
        return lax.ppermute(value, "segment", pairs)

    pair = range(2)
    e0 = run_block(weights[0], [(fields, None)], gains[0], edges)
    a0 = e0["out"]
    around = halo(e0)
    a1 = [
        run_block(weights[1], [(a0, m)], gains[1], edges, halo=[(side, m) for side in around])["out"] for m in pair
    ]
    skip = pass_on(a0, PAIRS)
    entering = [(pass_on(a1[m], PAIRS), None) for m in pair]
    e1 = run_block(weights[0], entering, gains[0], edges, skip=(skip, None))
    a2 = e1["out"]
    around = halo(e1)
    a3 = [
        run_block(weights[1], [(e1["joined"], m)], gains[1], edges, halo=[(side, m) for side in around])["out"]
        for m in pair
    ]

    down_out = pass_on(jnp.where(segment == 1, a0, jnp.concatenate(a1, axis=0)), [(0, 1), (1, 0)])
    up_out = [pass_on(jnp.where(segment == 3, a2[m : m + 1], a3[m]), [(2, 3), (3, 2)]) for m in pair]

    out = jnp.zeros((1, 4, LEVELS, 12, 6, D), jnp.bfloat16)

    def place_out(out, field, slot):
        field = field.reshape(1, 1, 2, LEVELS, 6, 6, D).transpose(0, 1, 3, 2, 4, 5, 6).reshape(1, 1, LEVELS, 12, 6, D)
        return lax.dynamic_update_slice(out, field, (0, slot, 0, 0, 0, 0))

    for m in pair:
        first_stage = jnp.where(segment == 0, a0[m : m + 1], a1[m])
        second_stage = jnp.where(segment == 2, a2[m : m + 1], a3[m])
        kept = jnp.where(segment < 2, first_stage, second_stage)
        out = place_out(out, kept, jnp.where(low, m, m + 2))
        got = jnp.where(segment < 2, down_out[m : m + 1], up_out[m])
        out = place_out(out, got, jnp.where(low, m + 2, m))
    return out


def solution(mesh):
    return jax.shard_map(
        on_device,
        mesh=mesh,
        in_specs=(
            P(None, None, "lat", None, None),
            P("segment", None, None),
            P("segment", "lat", None),
            P("segment", "lat", None),
            P("segment", "lat", None),
            P("segment", "lat", None),
        ),
        out_specs=P("segment", None, None, "lat", None, None),
        check_vma=False,
    )
```

```python
import jax
import jax.numpy as jnp
from jax import lax
from jax.experimental import pallas as pl
from jax.experimental.pallas import tpu as pltpu
from jax.sharding import PartitionSpec as P

D = 512
LEVELS = 4
HALFROWS = 144
OWN = 288
PER_LEVEL = 36
EPS = 1e-5


def layer_norm(wide, gain):
    center = jnp.mean(wide, axis=-1, keepdims=True)
    moved = wide - center
    spread = jnp.mean(moved * moved, axis=-1, keepdims=True)
    return moved * lax.rsqrt(spread + EPS) * gain


def dot(a, b):
    return jnp.dot(a, b, preferred_element_type=jnp.float32)


def attention(q, k, v, bias):
    rows, keys = q.shape[0], k.shape[0]
    first_lane = lax.broadcasted_iota(jnp.int32, (rows, 128), 1) < 64
    zero = jnp.zeros_like(q)
    stacked = jnp.concatenate([jnp.where(first_lane, q, zero), jnp.where(first_lane, zero, q)], axis=0)
    stacked = stacked.astype(jnp.bfloat16)
    k, v = k.astype(jnp.bfloat16), v.astype(jnp.bfloat16)
    scores = lax.dot_general(stacked, k, (((1,), (1,)), ((), ())), preferred_element_type=jnp.float32)
    if bias is not None:
        scores = scores + bias
    top = jnp.max(scores, axis=-1, keepdims=True)
    terms = jnp.exp2(scores - top).astype(jnp.bfloat16)
    both = dot(terms, jnp.concatenate([v, jnp.ones((keys, 128), jnp.bfloat16)], axis=1))
    weighed = jnp.where(first_lane, both[:rows, :128], both[rows:, :128])
    total = jnp.where(first_lane, both[:rows, 128:], both[rows:, 128:])
    return weighed / total


GROUP = 72


def group_bias(split, half, has_prev, has_next):
    row = lax.broadcasted_iota(jnp.int32, (2 * GROUP, 2 * GROUP), 0)
    col = lax.broadcasted_iota(jnp.int32, (2 * GROUP, 2 * GROUP), 1)
    far = col >= GROUP
    valid = (far | (has_prev > 0)) if half == 0 else (jnp.logical_not(far) | (has_next > 0))
    if split:
        query = jnp.where(row >= GROUP, row - GROUP, row) >= PER_LEVEL
        key = jnp.where(far, col - GROUP, col) >= PER_LEVEL
        valid = valid & (query == key)
    return jnp.where(valid, 0.0, -1e30).astype(jnp.float32)


def pairs_together(x):
    parts = [x[i : i + GROUP] for i in range(0, x.shape[0], GROUP)]
    return jnp.concatenate([parts[4 * (i // 4) + (0, 2, 1, 3)[i % 4]] for i in range(len(parts))], axis=0)


def turned(x, steps):
    halves = [x[i : i + HALFROWS] for i in range(0, x.shape[0], HALFROWS)]
    return jnp.concatenate([pltpu.roll(half, (steps * PER_LEVEL) % HALFROWS, 0) for half in halves], axis=0)


def block_kernel(shifted, joins, count, parts, edge_ref, refs, gain_ref, tiles, outs, mixed_ref):
    names = ("q", "k", "v", "proj", "up0", "up1", "up2", "up3")
    w = {name: (lambda i=i: tiles[i].reshape(D, D)) for i, name in enumerate(names)}

    def load(name):
        ref, index = refs[name]
        if index is None:
            return ref[...].reshape(-1, D).astype(jnp.float32)
        return ref[index].astype(jnp.float32)

    own = jnp.concatenate([load("own%d" % i) for i in range(parts)], axis=0)
    own = turned(own, -1) if shifted else pairs_together(own)
    gain0 = gain_ref[0:1, :]
    normed = layer_norm(own, gain0).astype(jnp.bfloat16)
    if shifted:
        before = layer_norm(turned(load("prev"), -1), gain0).astype(jnp.bfloat16)
        after = layer_norm(turned(load("next"), -1), gain0).astype(jnp.bfloat16)
        around = jnp.concatenate([before, normed, after], axis=0)
    else:
        around = normed
    q = dot(normed, w["q"]()) * (0.125 * 1.4426950408889634)
    k = dot(around, w["k"]())
    v = dot(around, w["v"]())
    columns = [slice(pair * 128, (pair + 1) * 128) for pair in range(4)]
    if shifted:
        for half in range(2):
            for group in range(2):
                bias = group_bias(group == 1, half, edge_ref[0], edge_ref[1])
                top = half * HALFROWS + group * GROUP
                near, far = half * OWN + group * GROUP, half * OWN + HALFROWS + group * GROUP
                for cols in columns:
                    keys, values = (
                        jnp.concatenate([x[near : near + GROUP, cols], x[far : far + GROUP, cols]], axis=0) for x in (k, v)
                    )
                    mixed_ref[top : top + GROUP, cols] = attention(q[top : top + GROUP, cols], keys, values, bias)
    else:
        for top in range(0, count * OWN, HALFROWS):
            rows = slice(top, top + HALFROWS)
            for cols in columns:
                mixed_ref[rows, cols] = attention(q[rows, cols], k[rows, cols], v[rows, cols], None)
    residual = own + dot(mixed_ref[...].astype(jnp.bfloat16), w["proj"]())
    inner = layer_norm(residual, gain_ref[1:2, :]).astype(jnp.bfloat16)
    total = residual
    for t in range(4):
        hidden = jax.nn.gelu(dot(inner, w["up%d" % t]())).astype(jnp.bfloat16)
        down = jnp.concatenate([tiles[8 + u, 8 * t + j] for j in range(8) for u in range(4)], axis=0)
        total = total + dot(hidden, down)
    result = (turned(total, 1) if shifted else pairs_together(total)).astype(jnp.bfloat16)
    outs["out"][...] = result.reshape(count, OWN, D)
    if joins:
        result = (result.astype(jnp.float32) + load("skip")).astype(jnp.bfloat16)
        outs["joined"][...] = result.reshape(count, OWN, D)
    if not shifted:
        whole = result.reshape(count, OWN, D)
        outs["top"][...] = whole[:, :HALFROWS]
        outs["bottom"][...] = whole[:, HALFROWS:]


ZS, YS = 8, 4
LATS = 2 * ZS * YS
PAIRS = [(0, 3), (1, 2)]


def run_block(weights, own, gains, edges, halo=None, skip=None):
    shifted = halo is not None
    joins = skip is not None
    operands = {"own%d" % i: field for i, field in enumerate(own)}
    count = sum(1 if index is not None else array.shape[0] for array, index in own)
    if shifted:
        operands["prev"], operands["next"] = halo
    if joins:
        operands["skip"] = skip
    names = list(operands)
    rows = {"out": OWN}
    if joins:
        rows["joined"] = OWN
    if not shifted:
        rows["top"] = rows["bottom"] = HALFROWS

    def body(edge_ref, gain_ref, tiles, *rest):
        refs = {name: (rest[i], operands[name][1]) for i, name in enumerate(names)}
        outs = dict(zip(rows, rest[len(names) :]))
        block_kernel(shifted, joins, count, len(own), edge_ref, refs, gain_ref, tiles, outs, rest[-1])

    vmem = pl.BlockSpec(memory_space=pltpu.VMEM)
    results = pl.pallas_call(
        body,
        out_shape=tuple(jax.ShapeDtypeStruct((count, n, D), jnp.bfloat16) for n in rows.values()),
        in_specs=[pl.BlockSpec(memory_space=pltpu.SMEM), vmem, vmem] + [vmem] * len(names),
        out_specs=(vmem,) * len(rows),
        scratch_shapes=[pltpu.VMEM((count * OWN, D), jnp.float32)],
        compiler_params=pltpu.CompilerParams(vmem_limit_bytes=(10 + 6 * count) * 1024 * 1024),
        cost_estimate=pl.CostEstimate(flops=count * 5 * 10**9, bytes_accessed=7 * 10**6, transcendentals=10**6),
    )(edges, gains, pltpu.with_memory_space_constraint(weights, pltpu.VMEM), *(operands[name][0] for name in names))
    return dict(zip(rows, results))


def pack(w_qkv, w_proj, w_up, w_down):
    def body(qkv, proj, up, down, out):
        wide = [qkv[...].astype(jnp.float32), proj[...].astype(jnp.float32), up[...].astype(jnp.float32)]
        parts = [wide[0][:, i * D : (i + 1) * D] for i in range(3)] + [wide[1]]
        parts += [wide[2][:, i * D : (i + 1) * D] for i in range(4)] + [down[...].astype(jnp.float32)]
        out[...] = jnp.concatenate(parts, axis=0).astype(jnp.bfloat16)

    vmem = pl.BlockSpec(memory_space=pltpu.VMEM)
    return pl.pallas_call(
        body,
        out_shape=jax.ShapeDtypeStruct((96, D), jnp.bfloat16),
        in_specs=[vmem] * 4,
        out_specs=vmem,
    )(w_qkv, w_proj, w_up, w_down)


def assemble(place, mine, passed, last_step):
    def body(place_ref, *rest):
        out, sems = rest[16], rest[17]
        z0, y0, core = place_ref[0], place_ref[1], place_ref[2]
        copies = []
        for side in range(2):
            source_core = core if side == 0 else 1 - core
            base = 6 * source_core
            for line, inners in enumerate(((0, -1), (1, last_step))):
                for piece, outer in enumerate((0, -1, 1, (-2, 2)[line])):
                    ref = rest[8 * side + 4 * line + piece]
                    for n, inner in enumerate(inners):
                        for far in range(2):
                            z_step = jnp.where(source_core == 0, inner, outer) + 4 * far
                            y_step = jnp.where(source_core == 0, outer, inner)
                            chip = lax.rem(z0 + z_step + ZS, ZS) * YS + lax.rem(y0 + y_step + YS, YS)
                            copy = pltpu.make_async_copy(
                                ref.at[n, far], out.at[pl.ds(base, 6), chip], sems.at[len(copies)]
                            )
                            copy.start()
                            copies.append(copy)
        for copy in copies:
            copy.wait()

    pieces = [*mine, *passed]
    for i in range(16):
        if i not in (11, 15):
            pieces[i] = pltpu.with_memory_space_constraint(pieces[i], pltpu.HBM)
    return pl.pallas_call(
        body,
        out_shape=pltpu.VMEM((12, 32, 16, D), jnp.bfloat16),
        in_specs=[pl.BlockSpec(memory_space=pltpu.SMEM)] + [pl.BlockSpec(memory_space=pl.ANY)] * 16,
        out_specs=pl.BlockSpec(memory_space=pltpu.VMEM),
        scratch_shapes=[pltpu.SemaphoreType.DMA((64,))],
        compiler_params=pltpu.CompilerParams(vmem_limit_bytes=16 * 1024 * 1024),
        cost_estimate=pl.CostEstimate(flops=10**9, bytes_accessed=6 * 10**6, transcendentals=0),
    )(place, *pieces)


def lat_id(z, y, core):
    return ((z % ZS) * YS + y % YS) * 2 + core


def moved(along):
    pairs = []
    for z in range(ZS):
        for y in range(YS):
            for core in range(2):
                dz, dy = along(core)
                pairs.append((lat_id(z, y, core), lat_id(z + dz, y + dy, core)))
    return pairs


def ring(level, step):
    return moved(lambda core: (step, 0) if (level == 0) == (core == 0) else (0, step))


SWAP = [(i, i ^ 1) for i in range(LATS)]


def send(value, pairs):
    return lax.ppermute(value, "lat", pairs)


def second_ring(first, second):
    near = [first, send(first, ring(1, 1)), send(first, ring(1, -1))]
    distant = [second, send(second, ring(1, 1)), send(second, ring(1, -1))]
    mine = near + [send(near[1], ring(1, 1))] + distant + [send(distant[2], ring(1, -1))]
    return mine, [send(piece, SWAP) for piece in mine]


def gather_weights(place, even, shard, early):
    both = jnp.stack([shard, send(shard, moved(lambda core: (4, 0)))])
    both, early = lax.optimization_barrier((both, early))
    other = lax.ppermute(both, "segment", [(0, 1), (1, 0), (2, 3), (3, 2)])
    base = jnp.stack([jnp.where(even, both, other), jnp.where(even, other, both)])
    before, after = send(base, ring(0, 1)), send(base, ring(0, -1))
    far = lax.optimization_barrier((send(before[0], ring(0, 1)), send(after[1], ring(0, -1))))
    lines = [(jnp.stack([base[b], before[b]]), jnp.stack([after[b], far[b]])) for b in range(2)]
    first = second_ring(*lines[0])
    first, line = lax.optimization_barrier((first, lines[1]))
    second = second_ring(*line)
    return [assemble(place, *first, -2), assemble(place, *second, 2)], early


def on_device(tokens, norm_gain, w_qkv, w_proj, w_up, w_down):
    segment = lax.axis_index("segment")
    lat = lax.axis_index("lat")
    core = lat % 2
    even = segment % 2 == 0
    low = (segment == 0) | (segment == 3)
    place = jnp.stack([lat // (2 * YS), (lat // 2) % YS, core]).astype(jnp.int32)
    edges = jnp.stack([lat > 0, lat < LATS - 1]).astype(jnp.int32)

    own = pack(w_qkv[0], w_proj[0], w_up[0], w_down[0])
    other = send(own, SWAP)
    first, second = jnp.where(core == 0, own, other), jnp.where(core == 0, other, own)
    tall = jnp.stack([first[:64].reshape(8, 8, D), second[:64].reshape(8, 8, D)], axis=1).reshape(8, 16, D)
    tall = jnp.concatenate([tall, first[64:].reshape(2, 16, D), second[64:].reshape(2, 16, D)], axis=0)
    shard = jnp.where(core == 0, tall[:6], tall[6:])
    other_gain = lax.ppermute(norm_gain[0], "segment", [(0, 1), (1, 0), (2, 3), (3, 2)])
    fields = jnp.where(low, tokens[:2], tokens[2:])
    fields = fields.reshape(2, LEVELS, 2, 6, 6, D).transpose(0, 2, 1, 3, 4, 5).reshape(2, OWN, D)
    weights, (other_gain, fields) = gather_weights(place, even, shard, (other_gain, fields))
    gains = [jnp.where(even, norm_gain[0], other_gain), jnp.where(even, other_gain, norm_gain[0])]

    def halo(block):
        up = send(block["bottom"], [(i, i + 1) for i in range(LATS - 1)])
        down = send(block["top"], [(i + 1, i) for i in range(LATS - 1)])
        return up, down

    def pass_on(value, pairs):
        return lax.ppermute(value, "segment", pairs)

    pair = range(2)
    e0 = run_block(weights[0], [(fields, None)], gains[0], edges)
    a0 = e0["out"]
    around = halo(e0)
    a1 = [
        run_block(weights[1], [(a0, m)], gains[1], edges, halo=[(side, m) for side in around])["out"] for m in pair
    ]
    skip = pass_on(a0, PAIRS)
    entering = [(pass_on(a1[m], PAIRS), None) for m in pair]
    e1 = run_block(weights[0], entering, gains[0], edges, skip=(skip, None))
    a2 = e1["out"]
    around = halo(e1)
    a3 = [
        run_block(weights[1], [(e1["joined"], m)], gains[1], edges, halo=[(side, m) for side in around])["out"]
        for m in pair
    ]

    down_out = pass_on(jnp.where(segment == 1, a0, jnp.concatenate(a1, axis=0)), [(0, 1), (1, 0)])
    up_out = [pass_on(jnp.where(segment == 3, a2[m : m + 1], a3[m]), [(2, 3), (3, 2)]) for m in pair]

    out = jnp.zeros((1, 4, LEVELS, 12, 6, D), jnp.bfloat16)

    def place_out(out, field, slot):
        field = field.reshape(1, 1, 2, LEVELS, 6, 6, D).transpose(0, 1, 3, 2, 4, 5, 6).reshape(1, 1, LEVELS, 12, 6, D)
        return lax.dynamic_update_slice(out, field, (0, slot, 0, 0, 0, 0))

    for m in pair:
        first_stage = jnp.where(segment == 0, a0[m : m + 1], a1[m])
        second_stage = jnp.where(segment == 2, a2[m : m + 1], a3[m])
        kept = jnp.where(segment < 2, first_stage, second_stage)
        out = place_out(out, kept, jnp.where(low, m, m + 2))
        got = jnp.where(segment < 2, down_out[m : m + 1], up_out[m])
        out = place_out(out, got, jnp.where(low, m + 2, m))
    return out


def solution(mesh):
    return jax.shard_map(
        on_device,
        mesh=mesh,
        in_specs=(
            P(None, None, "lat", None, None),
            P("segment", None, None),
            P("segment", "lat", None),
            P("segment", "lat", None),
            P("segment", "lat", None),
            P("segment", "lat", None),
        ),
        out_specs=P("segment", None, None, "lat", None, None),
        check_vma=False,
    )
```
